256 devices in a mesh: mp: 4 (over x), tok: 16 (over y, z_lo, core), col: 4 (over z_hi).
Axes of the slice: x: 4, y: 4, z: 8 (z_hi: 4, z_lo: 2; z = z_hi * 2 + z_lo), core: 2. Of those that a mesh axis runs over, the one named last changes fastest.
Arguments:
- ids: int32 [4, 8192], P('mp', 'tok'), may hold values from 0 to 151643, as said below
- hidden_in: bfloat16 [4, 8192, 3584], P('mp', 'tok'), may hold values from -6 to 6
- hidden_mid: bfloat16 [4, 8192, 3584], P('mp', 'tok'), may hold values from -6 to 6
- norm_gains: float32 [4, 2, 3584], P('mp'), may hold values from 0.25 to 4
- q_weight: bfloat16 [4, 3584, 3584], P('mp', 'col', 'tok'), may hold values from -0.09375 to 0.09375
- gate_weight: bfloat16 [4, 3584, 9472], P('mp', 'col', 'tok'), may hold values from -0.09375 to 0.09375
Outputs:
- gram_sums: float32 [2, 4, 16, 4, 14, 3584], P(None, 'mp', 'tok', 'col')
- query_numer: float32 [4, 16, 4, 14, 3584], P('mp', None, 'col', None, 'tok')
- gate_numer: float32 [4, 16, 4, 14, 9472], P('mp', None, 'col', None, 'tok')
The draws below stay inside these ranges and needn't reach their ends.
Inputs may be any that keep to these rules, and one draw needn't show every extreme that they name: Each calibration sequence of 256 consecutive tokens holds ids below 151643 from its start for one or more positions and the pad id 151643 at all later positions; every sequence ends in pad.
All inputs are finite; a program needn't handle non-finite values.
Results may differ from the reference program's by a relative error of at most 0.025.
Values may be sent and summed in bfloat16 or wider, within the bound.
No kernel may reach another device: no remote copies, remote signals or barrier semaphores. Data moves between devices by JAX's collectives and lax.ppermute only.
A program may use at most 256 MiB of HBM per device.

```python
import math
import jax
import jax.numpy as jnp
from jax import lax

D = 3584
FFW = 9472
SEQ = 256
TOK_DEV = 512
TOKENS = 8192
R = 14
N_MP = 4
N_TOK = 16
N_COL = 4


def draw_ids(key, part):
    key = jax.random.fold_in(key, 7)
    key_lengths, key_words = jax.random.split(key)
    count_seqs = TOKENS // SEQ
    seq_order = jnp.arange(count_seqs, dtype=jnp.int32)
    base_len = SEQ // 6 + seq_order * (2 * SEQ // 3) // count_seqs
    extra_len = jax.random.randint(key_lengths, (N_MP, count_seqs), 0, SEQ // 6 + 1)
    live_len = jnp.clip(base_len[None, :] + extra_len, 1, SEQ - 1)
    words = jax.random.randint(key_words, (N_MP, TOKENS), 0, 151643)
    positions = jnp.arange(TOKENS, dtype=jnp.int32)
    live_rows = jnp.repeat(live_len, SEQ, axis=1)
    return jnp.where((positions % SEQ)[None, :] < live_rows, words, 151643).astype(jnp.int32)


def raised(result, stream_key, source, target, shards_of, factor):
    owner, partner = [(jnp.arange(result.shape[axis_at]) // (result.shape[axis_at] // shards_of)).reshape([-1 if axis == axis_at else 1 for axis in range(result.ndim)]) for axis_at in (source, target)]
    chosen = jax.random.permutation(stream_key, shards_of)[partner]
    strong = (owner == chosen) | (owner == (partner + shards_of // 2) % shards_of)
    return jnp.where(strong, factor * result, result)


def levels(rng, extent, pieces, low, largest):
    loudness = 1.0
    for dim, blocks in pieces:
        heights = jax.random.uniform(jax.random.fold_in(jax.random.fold_in(rng, 6), dim), (blocks,), jnp.float32, low / len(pieces), largest / len(pieces))
        loudness = loudness * jnp.repeat(jnp.exp(heights), extent[dim] // blocks).reshape((-1,) + (1,) * (len(extent) - 1 - dim))
    return loudness


def scatter_about(own_key, shape, scale, most, cuts=(), kind=jnp.bfloat16):
    result = scale * jax.random.normal(own_key, shape, jnp.float32)
    if cuts:
        result = result * levels(own_key, shape, cuts, -0.22, 0.18)
    return jnp.clip(result, -most, most).astype(kind)


def noise_with(stream_key, shape, spread, most, cuts, heavy, kind=jnp.bfloat16):
    drawn = spread * jax.random.normal(stream_key, shape, jnp.float32)
    if cuts:
        drawn = drawn * levels(stream_key, shape, cuts, -0.22, 0.18)
    return jnp.clip(raised(drawn, jax.random.fold_in(stream_key, 3), *heavy), -most, most).astype(kind)


def setup_inputs(seed: int = 0) -> dict:
    key_of = jax.random.split(jax.random.key(seed), 7)
    ids = draw_ids(jax.random.fold_in(key_of[6], 71), 0)
    hidden_in = noise_with(key_of[1], (N_MP, TOKENS, D), 1.0, 6.0, ((0, 4), (1, 16)), (1, 2, 16, 2.0))
    hidden_mid = noise_with(key_of[2], (N_MP, TOKENS, D), 1.0, 6.0, ((0, 4), (1, 16)), (1, 2, 16, 2.0))
    norm_gains = jnp.clip(jnp.exp(math.log(4.0) - 2.7725887 * jax.random.uniform(key_of[3], (N_MP, 2, D), jnp.float32) ** levels(key_of[3], (N_MP, 2, D), ((0, 4),), -0.2, 0.2)), 0.25, 4.0)
    q_weight = scatter_about(key_of[4], (N_MP, D, D), D ** -0.5, 0.09375, ((0, 4), (1, 4), (2, 16)))
    gate_weight = scatter_about(key_of[5], (N_MP, D, FFW), D ** -0.5, 0.09375, ((0, 4), (1, 4), (2, 16)))
    return dict(ids=ids, hidden_in=hidden_in, hidden_mid=hidden_mid, norm_gains=norm_gains, q_weight=q_weight, gate_weight=gate_weight)


def normalize(hidden, gain):
    values = hidden.astype(jnp.float32)
    scale_rows = lax.rsqrt(lax.optimization_barrier(jnp.mean(values * values, axis=-1, keepdims=True)) + 1e-06)
    return (values * scale_rows * gain[None, :]).astype(jnp.bfloat16)

def block_gram(inputs, live_mask):
    masked = jnp.where(live_mask[:, None], inputs, jnp.zeros_like(inputs))
    blocks = inputs.reshape(N_TOK, TOK_DEV, inputs.shape[1])
    masked_blocks = masked.reshape(N_TOK, TOK_DEV, inputs.shape[1])

    def add_block(total, pair):
        plain, weighted = pair
        term = lax.dot_general(weighted, plain, (((0,), (0,)), ((), ())), preferred_element_type=jnp.float32)
        rounded = lax.optimization_barrier(term.astype(jnp.bfloat16))
        return (total + rounded.astype(jnp.float32), None)
    start = jnp.zeros((inputs.shape[1], inputs.shape[1]), jnp.float32)
    total, _ = lax.scan(add_block, start, (blocks, masked_blocks))
    return total

def reference(ids, hidden_in, hidden_mid, norm_gains, q_weight, gate_weight):
    width = hidden_in.shape[2]
    query_total = jnp.zeros((width, width), jnp.float32)
    gate_total = jnp.zeros((width, width), jnp.float32)
    query_prod = jnp.zeros((width, width), jnp.float32)
    gate_prod = jnp.zeros((width, gate_weight.shape[2]), jnp.float32)
    for model in range(N_MP):
        live_mask = ids[model] != 151643
        live_count = jnp.sum(live_mask.astype(jnp.float32))
        query_in = normalize(hidden_in[model], norm_gains[model, 0])
        gate_in = normalize(hidden_mid[model], norm_gains[model, 1])
        query_gram = (block_gram(query_in, live_mask) / live_count).astype(jnp.bfloat16)
        gate_gram = (block_gram(gate_in, live_mask) / live_count).astype(jnp.bfloat16)
        query_total = query_total + query_gram.astype(jnp.float32)
        gate_total = gate_total + gate_gram.astype(jnp.float32)
        query_term = jnp.dot(query_gram, q_weight[model], preferred_element_type=jnp.float32)
        gate_term = jnp.dot(gate_gram, gate_weight[model], preferred_element_type=jnp.float32)
        query_prod = query_prod + lax.optimization_barrier(query_term.astype(jnp.bfloat16)).astype(jnp.float32)
        gate_prod = gate_prod + lax.optimization_barrier(gate_term.astype(jnp.bfloat16)).astype(jnp.float32)
    gram_sums = jnp.stack([query_total, gate_total]).reshape(2, N_MP, N_TOK, N_COL, R, width)
    query_numer = query_prod.reshape(N_MP, N_TOK, N_COL, R, width)
    gate_numer = gate_prod.reshape(N_MP, N_TOK, N_COL, R, gate_weight.shape[2])
    return (gram_sums, query_numer, gate_numer)
```

```python
import functools

import jax
import jax.numpy as jnp
from jax import lax
from jax.experimental import pallas as pl
from jax.experimental.pallas import tpu as pltpu
from jax.sharding import PartitionSpec as P

PAD_ID = 151643
SLOTS = (0, 1, 3, 2)
VMEM = 48 * 1024 * 1024


def swap(value, axis, code):
    size = lax.axis_size(axis)
    return lax.ppermute(value, axis, [(i, i ^ code) for i in range(size)])


def total(*terms):
    out = terms[0].astype(jnp.float32)
    for term in terms[1:]:
        out = out + term.astype(jnp.float32)
    return out


def scatter_four(parts, axis, codes):
    one, three = codes
    first_two, second_two = parts[2]
    far_a = swap(total(*first_two).astype(jnp.bfloat16), axis, one)
    far_b = swap(total(*second_two).astype(jnp.bfloat16), axis, three)
    one_a = total(*parts[1][0]).astype(jnp.bfloat16)
    one_b = total(*parts[1][1], far_b).astype(jnp.bfloat16)
    three_a = total(*parts[3][0], far_a).astype(jnp.bfloat16)
    three_b = total(*parts[3][1]).astype(jnp.bfloat16)
    got_one = [swap(one_a, axis, one), swap(one_b, axis, one)]
    got_three = [swap(three_a, axis, three), swap(three_b, axis, three)]
    return tuple(
        list(parts[0][half]) + [got_one[half], got_three[half]] for half in range(2)
    )


def gram_kernel(place_ref, hidden_ref, live_ref, gain_ref, *rest, row_block, n_col):
    outs, (scale_ref, right_ref, acc_ref) = rest[:8], rest[8:]
    step = pl.program_id(0)
    width = hidden_ref.shape[2]
    chunk = right_ref.shape[1]
    piece = row_block * n_col
    tok = place_ref[1]

    def normed(start):
        start = pl.multiple_of(start, 128)
        values = hidden_ref[0, :, pl.ds(start, chunk)].astype(jnp.float32)
        gain = gain_ref[:, pl.ds(start, chunk)]
        return (values * scale_ref[...] * gain).astype(jnp.bfloat16)

    @pl.when(step == 0)
    def _():
        squares = jnp.zeros((hidden_ref.shape[1], 128), jnp.float32)
        for lane in range(0, width, 128):
            values = hidden_ref[0, :, lane : lane + 128].astype(jnp.float32)
            squares = squares + values * values
        mean = jnp.sum(squares, axis=1, keepdims=True) / width
        scale_ref[...] = lax.rsqrt(mean + 1e-06) * live_ref[...]
        right_ref[...] = normed(place_ref[2] * chunk)

    slot = jnp.where(step == 0, 0, jnp.where(step == 1, 1, jnp.where(step == 2, 3, 2)))
    left = normed((place_ref[0] ^ slot) * chunk)
    acc_ref[...] = lax.dot_general(
        left, right_ref[...], (((0,), (0,)), ((), ())), preferred_element_type=jnp.float32
    )
    for core in range(2):
        for at, y_slot in enumerate(SLOTS):
            for z_slot in range(2):
                source = (tok ^ (y_slot * 4 + z_slot * 2 + core)) * piece
                rows = acc_ref[pl.ds(pl.multiple_of(source, 8), piece), :]
                outs[core * 4 + at][0, z_slot] = rows.astype(jnp.bfloat16)


def gram_parts(place, hidden, live, gain, n_mp, n_col, row_block):
    tokens, width = hidden.shape[1:]
    chunk = width // n_mp
    piece = row_block * n_col
    out = jax.ShapeDtypeStruct((n_mp, 2, piece, chunk), jnp.bfloat16)
    return pl.pallas_call(
        functools.partial(gram_kernel, row_block=row_block, n_col=n_col),
        out_shape=[out] * 8,
        grid_spec=pltpu.PrefetchScalarGridSpec(
            num_scalar_prefetch=1,
            grid=(n_mp,),
            in_specs=[
                pl.BlockSpec((1, tokens, width), lambda i, place: (0, 0, 0)),
                pl.BlockSpec((tokens, 1), lambda i, place: (0, 0)),
                pl.BlockSpec((1, width), lambda i, place: (0, 0)),
            ],
            out_specs=[pl.BlockSpec((1, 2, piece, chunk), lambda i, place: (i, 0, 0, 0))] * 8,
            scratch_shapes=[
                pltpu.VMEM((tokens, 1), jnp.float32),
                pltpu.VMEM((tokens, chunk), jnp.bfloat16),
                pltpu.VMEM((chunk, chunk), jnp.float32),
            ],
        ),
        compiler_params=pltpu.CompilerParams(vmem_limit_bytes=VMEM),
        cost_estimate=pl.CostEstimate(
            flops=2 * tokens * width * chunk, bytes_accessed=10 * 2**20, transcendentals=tokens
        ),
    )(place, hidden, live, gain)


def numer_kernel(place_ref, *refs):
    out_ref = refs[4]
    for q_slot in range(4):
        for at, y_slot in enumerate(SLOTS):
            out_ref[place_ref[1] ^ (y_slot * 4 + q_slot)] = refs[q_slot][at].astype(jnp.float32)


def place_numer(place, pieces):
    _, rows, columns = pieces[0].shape
    return pl.pallas_call(
        numer_kernel,
        out_shape=jax.ShapeDtypeStruct((16, rows, columns), jnp.float32),
        in_specs=[pl.BlockSpec(memory_space=pltpu.SMEM)]
        + [pl.BlockSpec(memory_space=pltpu.VMEM)] * 4,
        out_specs=pl.BlockSpec(memory_space=pltpu.VMEM),
        compiler_params=pltpu.CompilerParams(vmem_limit_bytes=VMEM),
    )(place, *pieces)


def sums_kernel(place_ref, *refs):
    out_ref = refs[4]
    chunk = refs[0].shape[2]
    for slot in range(4):
        start = pl.multiple_of((place_ref[2] ^ slot) * chunk, 128)
        out_ref[:, :, pl.ds(start, chunk)] = refs[slot][...].astype(jnp.float32)


def place_sums(place, pieces):
    grams, rows, chunk = pieces[0].shape
    return pl.pallas_call(
        sums_kernel,
        out_shape=jax.ShapeDtypeStruct((grams, rows, 4 * chunk), jnp.float32),
        in_specs=[pl.BlockSpec(memory_space=pltpu.SMEM)]
        + [pl.BlockSpec(memory_space=pltpu.VMEM)] * 4,
        out_specs=pl.BlockSpec(memory_space=pltpu.VMEM),
        compiler_params=pltpu.CompilerParams(vmem_limit_bytes=VMEM),
    )(place, *pieces)


def finished_gram(parts, live_count):
    keep, send = parts[:4], parts[4:]
    order = (3, 1, 2, 0)
    got = {at: swap(send[at], "tok", 1) for at in order}
    addends = {}
    for at, slot in enumerate(SLOTS):
        addends[slot] = tuple([keep[at][h], got[at][h]] for h in (slice(0, 2), slice(2, 4)))
    own = scatter_four(addends, "tok", (4, 12))
    away = jnp.concatenate(
        [total(*[term[:, 1] for term in half]).astype(jnp.bfloat16) for half in own], axis=0
    )
    got_z = swap(away, "tok", 2)
    home = [
        total(*[term[:, 0] for term in half], got_z[at : at + 2])
        for at, half in zip((0, 2), own)
    ]
    return (jnp.concatenate(home, axis=0) / live_count).astype(jnp.bfloat16)


def gathered_gram(own):
    one = swap(own, "tok", 4)
    three = swap(own, "tok", 12)
    two_a = swap(one[:2], "tok", 12)
    two_b = swap(three[2:], "tok", 4)
    rows = []
    for at in range(4):
        two = two_a[at] if at < 2 else two_b[at - 2]
        rows.append(jnp.concatenate([own[at], one[at], three[at], two], axis=0))
    return rows


def gathered_weight(weight):
    far = swap(weight, "tok", 2)
    near = swap(weight, "tok", 1)
    both = swap(far, "tok", 1)
    return jnp.concatenate([weight, near, far, both], axis=1)


def products(gram_rows, weight, col_index, n_col, row_block):
    columns = weight.shape[1]
    parts = {}
    for slot in (2, 1, 3, 0):
        term = jnp.dot(
            gram_rows[SLOTS.index(slot)], weight, preferred_element_type=jnp.float32
        ).astype(jnp.bfloat16)
        half = term.shape[0] // 2
        parts[slot] = ([term[:half]], [term[half:]])
    halves = scatter_four(parts, "mp", (1, 3))
    summed = [
        total(*half).astype(jnp.bfloat16).reshape(2, n_col, row_block, columns) for half in halves
    ]
    parts = {
        slot: tuple(
            [lax.dynamic_index_in_dim(half, col_index ^ slot, 1, keepdims=False)]
            for half in summed
        )
        for slot in SLOTS
    }
    halves = scatter_four(parts, "col", (1, 3))
    mine = jnp.concatenate([total(*half).astype(jnp.bfloat16) for half in halves], axis=0)
    each = columns // 4
    pieces = [mine[:, :, :each]]
    for slot in (1, 2, 3):
        pieces.append(swap(mine[:, :, slot * each : (slot + 1) * each], "tok", slot))
    return pieces


def model_sums(query_own, gate_own, col_index, n_col, row_block):
    parts = {
        slot: ([query_own[at]], [gate_own[at]]) for at, slot in enumerate(SLOTS)
    }
    halves = scatter_four(parts, "mp", (1, 3))
    summed = jnp.stack([total(*half).astype(jnp.bfloat16) for half in halves])
    summed = summed.reshape(2, n_col, row_block, summed.shape[-1])
    pieces = []
    for slot in range(4):
        rows = lax.dynamic_index_in_dim(summed, col_index ^ slot, 1, keepdims=False)
        pieces.append(swap(rows, "col", slot) if slot else rows)
    return pieces


def body(ids, hidden_in, hidden_mid, norm_gains, q_weight, gate_weight):
    n_mp = lax.axis_size("mp")
    n_tok = lax.axis_size("tok")
    n_col = lax.axis_size("col")
    col_index = lax.axis_index("col")
    width = hidden_in.shape[2]
    row_block = width // (n_mp * n_tok * n_col)
    place = jnp.stack([lax.axis_index("mp"), lax.axis_index("tok"), col_index]).astype(jnp.int32)
    live = (ids[0] != PAD_ID).astype(jnp.float32)
    live_count = jnp.full((8, 128), jnp.sum(live))
    for code in (1, 2, 4, 8):
        live_count = live_count + swap(live_count, "tok", code)
    live_count = live_count[0, 0]
    live = live[:, None]
    gate_parts = gram_parts(place, hidden_mid, live, norm_gains[0, 1:2], n_mp, n_col, row_block)
    query_parts = gram_parts(place, hidden_in, live, norm_gains[0, 0:1], n_mp, n_col, row_block)
    gate_cols = gathered_weight(gate_weight[0])
    query_cols = gathered_weight(q_weight[0])
    gate_own = finished_gram(gate_parts, live_count)
    query_own = finished_gram(query_parts, live_count)
    gate_rows = gathered_gram(gate_own)
    query_rows = gathered_gram(query_own)
    gate_pieces = products(gate_rows, gate_cols, col_index, n_col, row_block)
    query_pieces = products(query_rows, query_cols, col_index, n_col, row_block)
    sum_pieces = model_sums(query_own, gate_own, col_index, n_col, row_block)
    gram_sums = place_sums(place, sum_pieces)
    query_numer = place_numer(place, query_pieces)
    gate_numer = place_numer(place, gate_pieces)
    return (
        gram_sums[:, None, None, None],
        query_numer[None, :, None],
        gate_numer[None, :, None],
    )


def solution(mesh):
    placed = (
        P("mp", "tok"),
        P("mp", "tok", None),
        P("mp", "tok", None),
        P("mp", None, None),
        P("mp", "col", "tok"),
        P("mp", "col", "tok"),
    )
    return jax.shard_map(
        body,
        mesh=mesh,
        in_specs=placed,
        out_specs=(
            P(None, "mp", "tok", "col", None, None),
            P("mp", None, "col", None, "tok"),
            P("mp", None, "col", None, "tok"),
        ),
        check_vma=False,
    )
```

```python
import functools

import jax
import jax.numpy as jnp
from jax import lax
from jax.experimental import pallas as pl
from jax.experimental.pallas import tpu as pltpu
from jax.sharding import PartitionSpec as P

PAD_ID = 151643
SLOTS = (0, 1, 3, 2)
VMEM = 48 * 1024 * 1024


def swap(value, axis, code):
    size = lax.axis_size(axis)
    return lax.ppermute(value, axis, [(i, i ^ code) for i in range(size)])


def total(*terms):
    out = terms[0].astype(jnp.float32)
    for term in terms[1:]:
        out = out + term.astype(jnp.float32)
    return out


def rounded(*terms, then=()):
    return (total(*terms) + nothing(*then)).astype(jnp.bfloat16)


def nothing(*values):
    zero = jnp.zeros((), jnp.float32)
    for value in values:
        zero = zero + value[(0,) * value.ndim].astype(jnp.float32) * 0.0
    return zero


def later(value, lead):
    return jnp.pad(value.astype(jnp.float32), ((lead, 0),) + ((0, 0),) * (value.ndim - 1))


def earlier(value, trail):
    return jnp.pad(value.astype(jnp.float32), ((0, trail),) + ((0, 0),) * (value.ndim - 1))


def pair(values, axis, codes):
    return tuple(swap(value, axis, code) for value, code in zip(values, codes))


class Order:
    def __init__(self, token):
        self.token = token

    def hold(self, *values):
        self.token, *out = lax.optimization_barrier((self.token, *values))
        return tuple(out)


def product_kernel(*refs, first, columns):
    rows, weights, outs, left_ref, right_ref = refs[:4], refs[4:8], refs[8:13], refs[13], refs[14]
    piece = rows[0].shape[1]
    pad = left_ref.shape[0] // 4
    for at in range(4):
        right_ref[at * columns : (at + 1) * columns, :] = weights[at][
            first : first + columns, :
        ]
    left_ref[...] = jnp.zeros_like(left_ref)
    for slot in (2, 1, 3, 0):
        for at in range(4):
            left_ref[at * pad : at * pad + piece, :] = rows[at][SLOTS.index(slot)]
        term = lax.dot_general(
            left_ref[...],
            right_ref[...],
            (((1,), (1,)), ((), ())),
            preferred_element_type=jnp.float32,
        )
        for at in range(4):
            block = term[at * pad : at * pad + piece, :].astype(jnp.bfloat16)
            if slot == 2:
                outs[at // 2][at % 2] = block
            else:
                outs[2 + (1, 3, 0).index(slot)][at] = block


def products(rows, weights, first, columns):
    piece, depth = rows[0].shape[1:]
    wide = 4 * columns
    half = jax.ShapeDtypeStruct((2, piece, wide), jnp.bfloat16)
    whole = jax.ShapeDtypeStruct((4, piece, wide), jnp.bfloat16)
    pad = -(-piece // 16) * 16
    return pl.pallas_call(
        functools.partial(product_kernel, first=first, columns=columns),
        out_shape=[half, half, whole, whole, whole],
        in_specs=[pl.BlockSpec(memory_space=pltpu.VMEM)] * 8,
        out_specs=[pl.BlockSpec(memory_space=pltpu.VMEM)] * 5,
        scratch_shapes=[
            pltpu.VMEM((4 * pad, depth), jnp.bfloat16),
            pltpu.VMEM((wide, depth), jnp.bfloat16),
        ],
        compiler_params=pltpu.CompilerParams(vmem_limit_bytes=VMEM),
        cost_estimate=pl.CostEstimate(
            flops=2 * 16 * pad * depth * wide, bytes_accessed=12 * 2**20, transcendentals=0
        ),
    )(*rows, *weights)


def last_of(one, three, far, then=()):
    half = far[0].shape[0]
    return (
        rounded(one, later(far[1], half), then=then),
        rounded(three, earlier(far[0], half), then=then),
    )


def ring_all(value, axis, codes):
    one, three = codes
    return (
        swap(value, axis, one),
        swap(value, axis, three),
        swap(value, axis, one ^ three),
    )


def row_sets(value, col_index, n_col, row_block):
    value = value.reshape(value.shape[0], n_col, row_block, value.shape[-1])
    return [
        lax.dynamic_index_in_dim(value, col_index ^ slot, 1, keepdims=False) for slot in range(4)
    ]


def column_blocks(value):
    each = value.shape[-1] // 4
    return [value[:, :, slot * each : (slot + 1) * each] for slot in range(4)]


def body(ids, hidden_in, hidden_mid, norm_gains, q_weight, gate_weight):
    n_mp = lax.axis_size("mp")
    n_tok = lax.axis_size("tok")
    n_col = lax.axis_size("col")
    col_index = lax.axis_index("col")
    width = hidden_in.shape[2]
    row_block = width // (n_mp * n_tok * n_col)
    piece = row_block * n_col
    place = jnp.stack([lax.axis_index("mp"), lax.axis_index("tok"), col_index]).astype(jnp.int32)
    y_codes, ring_codes = (4, 12), (1, 3)
    order = Order(place)
    hold = order.hold
    n_gate, n_query = gate_weight.shape[2], q_weight.shape[2]

    def core_parts(keep, got):
        return {slot: (keep[at], got[at]) for at, slot in enumerate(SLOTS)}

    def y_far(parts):
        return (
            rounded(*[term[:1] for term in parts[2]]),
            rounded(*[term[1:] for term in parts[2]]),
        )

    def y_last(parts, far, then=()):
        return (
            rounded(*parts[1], later(far[1], 1), then=then),
            rounded(*parts[3], earlier(far[0], 1), then=then),
        )

    def away_rows(parts, last):
        return rounded(*[term[1] for term in (*parts[0], *last)])

    def home_rows(parts, last, got, then=()):
        home = total(*[term[0] for term in (*parts[0], *last)], got) + nothing(*then)
        return (home / count[0, 0]).astype(jnp.bfloat16)

    weight = jnp.concatenate([gate_weight[0].T, q_weight[0].T], axis=0)
    weight_far = swap(weight, "tok", 2)
    gate_keep, gate_send, count = hold(
        *gram_parts(place, hidden_mid, ids, norm_gains, 1, n_mp, piece)
    )
    gate_got = swap(gate_send, "tok", 1)
    query_place = place + (count[0, :3] * 0.0).astype(jnp.int32)
    query_keep, query_send, _ = hold(
        *gram_parts(query_place, hidden_in, ids, norm_gains, 0, n_mp, piece)
    )
    (gate_got,) = hold(gate_got)
    gate_parts = core_parts(gate_keep, gate_got)
    far = hold(*y_far(gate_parts))
    gate_far = pair(far, "tok", y_codes)
    count_got = swap(count + nothing(far[1]), "tok", 1)
    query_got = swap(query_send, "tok", 1)
    (query_got,) = hold(query_got)
    query_parts = core_parts(query_keep, query_got)
    early = hold(*y_far(query_parts))
    *gate_far, count_got = hold(*gate_far, count_got)
    *last, count = hold(*y_last(gate_parts, gate_far), count + count_got)
    count_got = swap(count, "tok", 4)
    gate_last = pair(last, "tok", y_codes)
    count = count + count_got
    count_got = swap(count, "tok", 12)
    weight_near = swap(weight, "tok", 1)
    *gate_last, count_got = hold(*gate_last, count_got)
    away, count, *early = hold(away_rows(gate_parts, gate_last), count + count_got, *early)
    gate_got = swap(away, "tok", 2)
    count_got = swap(count, "tok", 2)
    weight_far = rounded(weight_far, then=(away,))
    weights = [weight, weight_near, weight_far, swap(weight_far, "tok", 1)]
    query_far = pair(early, "tok", y_codes)
    gate_got, count_got = hold(gate_got, count_got)
    count = count + count_got
    query_far = hold(*query_far)
    gate_own, count = hold(home_rows(gate_parts, gate_last, gate_got, query_far[1:]), count)
    gate_ring = ring_all(gate_own, "tok", y_codes)
    gate_ring = hold(*gate_ring)
    last = hold(*y_last(query_parts, query_far, gate_ring[2:]))
    query_last = pair(last, "tok", y_codes)
    far_a, far_b, one, three, gate_home = hold(
        *products((gate_own, *gate_ring), weights, 0, n_gate)
    )
    gate_far = pair((far_a, far_b), "mp", ring_codes)
    gate_far = hold(*gate_far)
    last = hold(*last_of(one, three, gate_far))
    gate_last = pair(last, "mp", ring_codes)
    query_last = hold(*query_last)
    (away,) = hold(away_rows(query_parts, query_last))
    query_got = swap(away, "tok", 2)
    (query_got,) = hold(query_got)
    (query_own,) = hold(home_rows(query_parts, query_last, query_got, last[1:]))
    query_ring = ring_all(query_own, "tok", y_codes)
    sums = hold(*[jnp.stack([query_own[at], gate_own[at]]) for at in range(4)])
    sums_got = [swap(sums[at], "mp", SLOTS[at]) for at in (1, 2, 3)]
    gate_last = hold(*gate_last)
    parts = row_sets(rounded(gate_home, *gate_last), col_index, n_col, row_block)
    gate_home, *parts = hold(*parts)
    gate_zh = parts
    gate_got = [swap(parts[slot - 1], "col", slot) for slot in (2, 1, 3)]
    query_ring = hold(*query_ring)
    far_a, far_b, one, three, query_home = hold(
        *products((query_own, *query_ring), weights, n_gate, n_query)
    )
    query_far = pair((far_a, far_b), "mp", ring_codes)
    sums_got = hold(*sums_got)
    parts = hold(*row_sets(rounded(sums[0], *sums_got), col_index, n_col, row_block))
    sum_pieces = [parts[0]] + [swap(parts[slot], "col", slot) for slot in (1, 2, 3)]
    query_far = hold(*query_far)
    last = hold(*last_of(one, three, query_far, gate_zh[:1]))
    query_last = pair(last, "mp", ring_codes)
    query_last = hold(*query_last)
    parts = row_sets(rounded(query_home, *query_last, then=(gate_zh[0],)), col_index, n_col, row_block)
    query_home, *parts = hold(*parts)
    query_got = [swap(parts[slot - 1], "col", slot) for slot in (2, 1, 3)]
    gate_got = hold(*gate_got)
    parts = hold(*column_blocks(rounded(gate_home, *gate_got)))
    gate_pieces = [parts[0]] + [swap(parts[slot], "tok", slot) for slot in (1, 2, 3)]
    sum_pieces = hold(*sum_pieces)
    (gram_sums,) = hold(place_sums(place, sum_pieces))
    query_got = hold(*query_got)
    parts = hold(*column_blocks(rounded(query_home, *query_got)))
    query_pieces = [parts[0]] + [swap(parts[slot], "tok", slot) for slot in (1, 2, 3)]
    gate_pieces = hold(*gate_pieces)
    (gate_numer,) = hold(place_numer(place, gate_pieces))
    query_pieces = hold(*query_pieces)
    query_numer = place_numer(place, query_pieces)
    return (
        gram_sums[:, None, None, None],
        query_numer[None, :, None],
        gate_numer[None, :, None],
    )


def gram_kernel(place_ref, hidden_ref, ids_ref, gain_ref, *rest, piece, gain_row):
    (keep_ref, send_ref, count_ref), (scale_ref, right_ref, acc_ref) = rest[:3], rest[3:]
    step = pl.program_id(0)
    width = hidden_ref.shape[2]
    chunk = right_ref.shape[1]
    tok = place_ref[1]

    def normed(start):
        start = pl.multiple_of(start, 128)
        values = hidden_ref[0, :, pl.ds(start, chunk)].astype(jnp.float32)
        gain = gain_ref[0, gain_row : gain_row + 1, pl.ds(start, chunk)]
        return (values * scale_ref[...] * gain).astype(jnp.bfloat16)

    @pl.when(step == 0)
    def _():
        squares = jnp.zeros((hidden_ref.shape[1], 128), jnp.float32)
        for lane in range(0, width, 128):
            values = hidden_ref[0, :, lane : lane + 128].astype(jnp.float32)
            squares = squares + values * values
        mean = jnp.sum(squares, axis=1, keepdims=True) / width
        live = (ids_ref[...] != PAD_ID).astype(jnp.float32)
        count_ref[...] = jnp.full(count_ref.shape, jnp.sum(live))
        live = jnp.broadcast_to(live, (128, live.shape[1])).T[:, :1]
        scale_ref[...] = lax.rsqrt(mean + 1e-06) * live
        right_ref[...] = normed(place_ref[2] * chunk)

    slot = jnp.where(step == 0, 0, jnp.where(step == 1, 1, jnp.where(step == 2, 3, 2)))
    left = normed((place_ref[0] ^ slot) * chunk)
    acc_ref[...] = lax.dot_general(
        left, right_ref[...], (((0,), (0,)), ((), ())), preferred_element_type=jnp.float32
    )
    for core, out_ref in enumerate((keep_ref, send_ref)):
        for at, y_slot in enumerate(SLOTS):
            for z_slot in range(2):
                source = (tok ^ (y_slot * 4 + z_slot * 2 + core)) * piece
                rows = acc_ref[pl.ds(pl.multiple_of(source, 8), piece), :]
                out_ref[at, z_slot, 0] = rows.astype(jnp.bfloat16)


def gram_parts(place, hidden, ids, gain, gain_row, n_mp, piece):
    tokens, width = hidden.shape[1:]
    chunk = width // n_mp
    out = jax.ShapeDtypeStruct((4, 2, n_mp, piece, chunk), jnp.bfloat16)
    return pl.pallas_call(
        functools.partial(gram_kernel, piece=piece, gain_row=gain_row),
        out_shape=[out, out, jax.ShapeDtypeStruct((8, 128), jnp.float32)],
        grid_spec=pltpu.PrefetchScalarGridSpec(
            num_scalar_prefetch=1,
            grid=(n_mp,),
            in_specs=[
                pl.BlockSpec((1, tokens, width), lambda i, place: (0, 0, 0)),
                pl.BlockSpec((1, tokens), lambda i, place: (0, 0)),
                pl.BlockSpec((1, 2, width), lambda i, place: (0, 0, 0)),
            ],
            out_specs=[
                pl.BlockSpec((4, 2, 1, piece, chunk), lambda i, place: (0, 0, i, 0, 0))
            ]
            * 2
            + [pl.BlockSpec((8, 128), lambda i, place: (0, 0))],
            scratch_shapes=[
                pltpu.VMEM((tokens, 1), jnp.float32),
                pltpu.VMEM((tokens, chunk), jnp.bfloat16),
                pltpu.VMEM((chunk, chunk), jnp.float32),
            ],
        ),
        compiler_params=pltpu.CompilerParams(vmem_limit_bytes=VMEM),
        cost_estimate=pl.CostEstimate(
            flops=2 * tokens * width * chunk, bytes_accessed=10 * 2**20, transcendentals=tokens
        ),
    )(place, hidden, ids, gain)


def numer_kernel(place_ref, *refs):
    out_ref = refs[4]
    for q_slot in range(4):
        for at, y_slot in enumerate(SLOTS):
            out_ref[place_ref[1] ^ (y_slot * 4 + q_slot)] = refs[q_slot][at].astype(jnp.float32)


def place_numer(place, pieces):
    _, rows, columns = pieces[0].shape
    return pl.pallas_call(
        numer_kernel,
        out_shape=jax.ShapeDtypeStruct((16, rows, columns), jnp.float32),
        in_specs=[pl.BlockSpec(memory_space=pltpu.SMEM)]
        + [pl.BlockSpec(memory_space=pltpu.VMEM)] * 4,
        out_specs=pl.BlockSpec(memory_space=pltpu.VMEM),
        compiler_params=pltpu.CompilerParams(vmem_limit_bytes=VMEM),
    )(place, *pieces)


def sums_kernel(place_ref, *refs):
    out_ref = refs[4]
    chunk = refs[0].shape[2]
    for slot in range(4):
        start = pl.multiple_of((place_ref[2] ^ slot) * chunk, 128)
        out_ref[:, :, pl.ds(start, chunk)] = refs[slot][...].astype(jnp.float32)


def place_sums(place, pieces):
    grams, rows, chunk = pieces[0].shape
    return pl.pallas_call(
        sums_kernel,
        out_shape=jax.ShapeDtypeStruct((grams, rows, 4 * chunk), jnp.float32),
        in_specs=[pl.BlockSpec(memory_space=pltpu.SMEM)]
        + [pl.BlockSpec(memory_space=pltpu.VMEM)] * 4,
        out_specs=pl.BlockSpec(memory_space=pltpu.VMEM),
        compiler_params=pltpu.CompilerParams(vmem_limit_bytes=VMEM),
    )(place, *pieces)


def solution(mesh):
    placed = (
        P("mp", "tok"),
        P("mp", "tok", None),
        P("mp", "tok", None),
        P("mp", None, None),
        P("mp", "col", "tok"),
        P("mp", "col", "tok"),
    )
    return jax.shard_map(
        body,
        mesh=mesh,
        in_specs=placed,
        out_specs=(
            P(None, "mp", "tok", "col", None, None),
            P("mp", None, "col", None, "tok"),
            P("mp", None, "col", None, "tok"),
        ),
        check_vma=False,
    )
```

```python
import functools

import jax
import jax.numpy as jnp
from jax import lax
from jax.experimental import pallas as pl
from jax.experimental.pallas import tpu as pltpu
from jax.sharding import PartitionSpec as P

PAD_ID = 151643
SLOTS = (0, 1, 3, 2)
VMEM = 48 * 1024 * 1024


def swap(value, axis, code):
    size = lax.axis_size(axis)
    return lax.ppermute(value, axis, [(i, i ^ code) for i in range(size)])


def total(*terms):
    out = terms[0].astype(jnp.float32)
    for term in terms[1:]:
        out = out + term.astype(jnp.float32)
    return out


def rounded(*terms, then=()):
    return (total(*terms) + nothing(*then)).astype(jnp.bfloat16)


def nothing(*values):
    zero = jnp.zeros((), jnp.float32)
    for value in values:
        zero = zero + value[(0,) * value.ndim].astype(jnp.float32) * 0.0
    return zero


def later(value, lead):
    return jnp.pad(value.astype(jnp.float32), ((lead, 0),) + ((0, 0),) * (value.ndim - 1))


def earlier(value, trail):
    return jnp.pad(value.astype(jnp.float32), ((0, trail),) + ((0, 0),) * (value.ndim - 1))


def pair(values, axis, codes):
    return tuple(swap(value, axis, code) for value, code in zip(values, codes))


class Order:
    def __init__(self, token):
        self.token = token

    def hold(self, *values):
        self.token, *out = lax.optimization_barrier((self.token, *values))
        return tuple(out)


def product_kernel(place_ref, *refs, first, columns, n_col):
    rows, weights, outs, (left_ref, right_ref) = refs[:5], refs[5:9], refs[9:14], refs[14:]
    piece, depth = rows[0].shape[1:]
    pad = left_ref.shape[0] // 4
    block = piece // n_col
    wide = 4 * columns
    share = depth // 4
    for at in range(4):
        right_ref[at * columns : (at + 1) * columns, :] = weights[at][
            first : first + columns, :
        ]
    left_ref[...] = jnp.zeros_like(left_ref)
    for slot in (2, 1, 3, 0):
        position = SLOTS.index(slot)
        for at in range(3):
            left_ref[at * pad : at * pad + piece, :] = rows[at][position]
        left_ref[3 * pad : 3 * pad + piece, :] = rows[3 + position // 2][position % 2]
        term = lax.dot_general(
            left_ref[...],
            right_ref[...],
            (((1,), (1,)), ((), ())),
            preferred_element_type=jnp.float32,
        )
        own = rows[0][position].astype(jnp.float32)
        for col in range(n_col):
            held = place_ref[2] ^ col
            if slot == 2:
                out_ref, index = None, held
            else:
                out_ref, index = outs[2 + (1, 3, 0).index(slot)], held
            start = col * block
            product = jnp.concatenate(
                [term[at * pad + start : at * pad + start + block] for at in range(4)], axis=0
            ).astype(jnp.bfloat16)
            gram = jnp.concatenate(
                [
                    own[start : start + block, at * share : (at + 1) * share]
                    for at in range(4)
                ],
                axis=0,
            ).astype(jnp.bfloat16)
            if slot == 2:
                for half in range(2):

                    @pl.when(index // 2 == half)
                    def _(half=half, product=product, gram=gram, index=index):
                        outs[half][index % 2, :, :wide] = product
                        outs[half][index % 2, :, wide:] = gram

            else:
                out_ref[index, :, :wide] = product
                out_ref[index, :, wide:] = gram


def products(place, rows, weights, first, columns, n_col):
    piece, depth = rows[0].shape[1:]
    wide = 4 * columns
    half = jax.ShapeDtypeStruct((2, piece, wide + depth // 4), jnp.bfloat16)
    whole = jax.ShapeDtypeStruct((4, piece, wide + depth // 4), jnp.bfloat16)
    pad = -(-piece // 16) * 16
    return pl.pallas_call(
        functools.partial(product_kernel, first=first, columns=columns, n_col=n_col),
        out_shape=[half, half, whole, whole, whole],
        in_specs=[pl.BlockSpec(memory_space=pltpu.SMEM)]
        + [pl.BlockSpec(memory_space=pltpu.VMEM)] * 9,
        out_specs=[pl.BlockSpec(memory_space=pltpu.VMEM)] * 5,
        scratch_shapes=[
            pltpu.VMEM((4 * pad, depth), jnp.bfloat16),
            pltpu.VMEM((wide, depth), jnp.bfloat16),
        ],
        compiler_params=pltpu.CompilerParams(vmem_limit_bytes=VMEM),
        cost_estimate=pl.CostEstimate(
            flops=2 * 16 * pad * depth * wide, bytes_accessed=12 * 2**20, transcendentals=0
        ),
    )(place, *rows, *weights)


def last_of(one, three, far, then=()):
    half = far[0].shape[0]
    return (
        rounded(one, later(far[1], half), then=then),
        rounded(three, earlier(far[0], half), then=then),
    )


def ring_all(value, axis, codes):
    half = value.shape[0] // 2
    near = pair((value, value), axis, codes)
    return (*near, *pair((near[1][:half], near[0][half:]), axis, codes))


def column_blocks(home, got, wide):
    value = rounded(*[term[:, :wide] for term in (home, *got)])
    each = wide // 4
    return [value[:, slot * each : (slot + 1) * each] for slot in range(4)]


def body(ids, hidden_in, hidden_mid, norm_gains, q_weight, gate_weight):
    n_mp = lax.axis_size("mp")
    n_tok = lax.axis_size("tok")
    n_col = lax.axis_size("col")
    col_index = lax.axis_index("col")
    width = hidden_in.shape[2]
    row_block = width // (n_mp * n_tok * n_col)
    piece = row_block * n_col
    place = jnp.stack([lax.axis_index("mp"), lax.axis_index("tok"), col_index]).astype(jnp.int32)
    y_codes, ring_codes = (4, 12), (1, 3)
    order = Order(place)
    hold = order.hold
    n_gate, n_query = gate_weight.shape[2], q_weight.shape[2]

    def core_parts(keep, got):
        return {slot: (keep[at], got[at]) for at, slot in enumerate(SLOTS)}

    def y_far(parts):
        return (
            rounded(*[term[:1] for term in parts[2]]),
            rounded(*[term[1:] for term in parts[2]]),
        )

    def y_last(parts, far, then=()):
        return (
            rounded(*parts[1], later(far[1], 1), then=then),
            rounded(*parts[3], earlier(far[0], 1), then=then),
        )

    def away_rows(parts, last):
        return rounded(*[term[1] for term in (*parts[0], *last)])

    def home_rows(parts, last, got, then=()):
        home = total(*[term[0] for term in (*parts[0], *last)], got) + nothing(*then)
        return (home / count[0, 0]).astype(jnp.bfloat16)

    weight = jnp.concatenate([gate_weight[0].T, q_weight[0].T], axis=0)
    weight_far = swap(weight, "tok", 2)
    gate_keep, gate_send, count = hold(
        *gram_parts(place, hidden_mid, ids, norm_gains, 1, n_mp, piece)
    )
    gate_got = swap(gate_send, "tok", 1)
    query_place = place + (count[0, :3] * 0.0).astype(jnp.int32)
    query_keep, query_send, _ = hold(
        *gram_parts(query_place, hidden_in, ids, norm_gains, 0, n_mp, piece)
    )
    (gate_got,) = hold(gate_got)
    gate_parts = core_parts(gate_keep, gate_got)
    far = hold(*y_far(gate_parts))
    gate_far = pair(far, "tok", y_codes)
    count = count + nothing(far[1])
    count = count + swap(count, "tok", 1)
    count_got = swap(count, "tok", 4)
    query_got = swap(query_send, "tok", 1)
    (query_got,) = hold(query_got)
    query_parts = core_parts(query_keep, query_got)
    early = hold(*y_far(query_parts))
    *gate_far, count_got = hold(*gate_far, count_got)
    *last, count = hold(*y_last(gate_parts, gate_far), count + count_got)
    gate_last = pair(last, "tok", y_codes)
    weight_near = swap(weight, "tok", 1)
    count_got = swap(count, "tok", 12)
    *gate_last, count_got = hold(*gate_last, count_got)
    away, count, *early = hold(away_rows(gate_parts, gate_last), count + count_got, *early)
    gate_got = swap(away, "tok", 2)
    count_got = swap(count, "tok", 2)
    weight_far = rounded(weight_far, then=(away,))
    weights = [weight, weight_near, weight_far, swap(weight_far, "tok", 1)]
    query_far = pair(early, "tok", y_codes)
    gate_got, count_got = hold(gate_got, count_got)
    count = count + count_got
    query_far = hold(*query_far)
    gate_own, count = hold(home_rows(gate_parts, gate_last, gate_got, query_far[1:]), count)
    gate_ring = ring_all(gate_own, "tok", y_codes)
    gate_ring = hold(*gate_ring)
    last = hold(*y_last(query_parts, query_far, gate_ring[3:]))
    query_last = pair(last, "tok", y_codes)
    far_a, far_b, one, three, gate_home = hold(
        *products(place, (gate_own, *gate_ring), weights, 0, n_gate, n_col)
    )
    gate_far = pair((far_a, far_b), "mp", ring_codes)
    gate_far = hold(*gate_far)
    last = hold(*last_of(one, three, gate_far))
    gate_last = pair(last, "mp", ring_codes)
    query_last = hold(*query_last)
    (away,) = hold(away_rows(query_parts, query_last))
    query_got = swap(away, "tok", 2)
    (query_got,) = hold(query_got)
    (query_own,) = hold(home_rows(query_parts, query_last, query_got, last[1:]))
    query_ring = ring_all(query_own, "tok", y_codes)
    gate_last = hold(*gate_last)
    gate_home, *parts = hold(*[rounded(*[v[at] for v in (gate_home, *gate_last)]) for at in range(4)])
    gate_zh = parts
    gate_got = [swap(parts[slot - 1], "col", slot) for slot in (2, 1, 3)]
    query_ring = hold(*query_ring)
    far_a, far_b, one, three, query_home = hold(
        *products(place, (query_own, *query_ring), weights, n_gate, n_query, n_col)
    )
    query_far = pair((far_a, far_b), "mp", ring_codes)
    query_far = hold(*query_far)
    last = hold(*last_of(one, three, query_far, gate_zh[:1]))
    query_last = pair(last, "mp", ring_codes)
    query_last = hold(*query_last)
    query_home, *parts = hold(*[rounded(*[v[at] for v in (query_home, *query_last)]) for at in range(4)])
    query_got = [swap(parts[slot - 1], "col", slot) for slot in (2, 1, 3)]
    gate_got = hold(*gate_got)
    parts = hold(*column_blocks(gate_home, gate_got, 4 * n_gate))
    gate_pieces = [parts[0]] + [swap(parts[slot], "tok", slot) for slot in (1, 2, 3)]
    query_got = hold(*query_got)
    parts = hold(*column_blocks(query_home, query_got, 4 * n_query))
    query_pieces = [parts[0]] + [swap(parts[slot], "tok", slot) for slot in (1, 2, 3)]
    gate_pieces = hold(*gate_pieces)
    (gate_numer,) = hold(place_numer(place, gate_pieces))
    sum_pieces = [value[:, 4 * n_query :] for value in (query_home, *query_got)]
    sum_pieces += [value[:, 4 * n_gate :] for value in (gate_home, *gate_got)]
    sum_pieces = [sum_pieces[at] for at in (0, 2, 1, 3, 4, 6, 5, 7)]
    (gram_sums,) = hold(place_sums(place, sum_pieces))
    query_pieces = hold(*query_pieces)
    query_numer = place_numer(place, query_pieces)
    return (
        gram_sums[:, None, None, None],
        query_numer[None, :, None],
        gate_numer[None, :, None],
    )


def gram_kernel(place_ref, hidden_ref, ids_ref, gain_ref, *rest, piece, gain_row):
    (keep_ref, send_ref, count_ref), (scale_ref, right_ref, acc_ref) = rest[:3], rest[3:]
    step = pl.program_id(0)
    width = hidden_ref.shape[2]
    chunk = right_ref.shape[1]
    tok = place_ref[1]

    def normed(start):
        start = pl.multiple_of(start, 128)
        values = hidden_ref[0, :, pl.ds(start, chunk)].astype(jnp.float32)
        gain = gain_ref[0, gain_row : gain_row + 1, pl.ds(start, chunk)]
        return (values * scale_ref[...] * gain).astype(jnp.bfloat16)

    @pl.when(step == 0)
    def _():
        squares = jnp.zeros((hidden_ref.shape[1], 128), jnp.float32)
        for lane in range(0, width, 128):
            values = hidden_ref[0, :, lane : lane + 128].astype(jnp.float32)
            squares = squares + values * values
        mean = jnp.sum(squares, axis=1, keepdims=True) / width
        live = (ids_ref[...] != PAD_ID).astype(jnp.float32)
        count_ref[...] = jnp.full(count_ref.shape, jnp.sum(live))
        live = jnp.broadcast_to(live, (128, live.shape[1])).T[:, :1]
        scale_ref[...] = lax.rsqrt(mean + 1e-06) * live
        right_ref[...] = normed(place_ref[2] * chunk)

    slot = jnp.where(step == 0, 0, jnp.where(step == 1, 1, jnp.where(step == 2, 3, 2)))
    left = normed((place_ref[0] ^ slot) * chunk)
    acc_ref[...] = lax.dot_general(
        left, right_ref[...], (((0,), (0,)), ((), ())), preferred_element_type=jnp.float32
    )
    for core, out_ref in enumerate((keep_ref, send_ref)):
        for at, y_slot in enumerate(SLOTS):
            for z_slot in range(2):
                source = (tok ^ (y_slot * 4 + z_slot * 2 + core)) * piece
                rows = acc_ref[pl.ds(pl.multiple_of(source, 8), piece), :]
                out_ref[at, z_slot, 0] = rows.astype(jnp.bfloat16)


def gram_parts(place, hidden, ids, gain, gain_row, n_mp, piece):
    tokens, width = hidden.shape[1:]
    chunk = width // n_mp
    out = jax.ShapeDtypeStruct((4, 2, n_mp, piece, chunk), jnp.bfloat16)
    return pl.pallas_call(
        functools.partial(gram_kernel, piece=piece, gain_row=gain_row),
        out_shape=[out, out, jax.ShapeDtypeStruct((8, 128), jnp.float32)],
        grid_spec=pltpu.PrefetchScalarGridSpec(
            num_scalar_prefetch=1,
            grid=(n_mp,),
            in_specs=[
                pl.BlockSpec((1, tokens, width), lambda i, place: (0, 0, 0)),
                pl.BlockSpec((1, tokens), lambda i, place: (0, 0)),
                pl.BlockSpec((1, 2, width), lambda i, place: (0, 0, 0)),
            ],
            out_specs=[
                pl.BlockSpec((4, 2, 1, piece, chunk), lambda i, place: (0, 0, i, 0, 0))
            ]
            * 2
            + [pl.BlockSpec((8, 128), lambda i, place: (0, 0))],
            scratch_shapes=[
                pltpu.VMEM((tokens, 1), jnp.float32),
                pltpu.VMEM((tokens, chunk), jnp.bfloat16),
                pltpu.VMEM((chunk, chunk), jnp.float32),
            ],
        ),
        compiler_params=pltpu.CompilerParams(vmem_limit_bytes=VMEM),
        cost_estimate=pl.CostEstimate(
            flops=2 * tokens * width * chunk, bytes_accessed=10 * 2**20, transcendentals=tokens
        ),
    )(place, hidden, ids, gain)


def numer_kernel(place_ref, *refs):
    out_ref = refs[4]
    rows = out_ref.shape[1]
    for q_slot in range(4):
        value = refs[q_slot][...].astype(jnp.float32)
        for at, y_slot in enumerate(SLOTS):
            out_ref[place_ref[1] ^ (y_slot * 4 + q_slot)] = value[at * rows : (at + 1) * rows]


def place_numer(place, pieces):
    rows, columns = pieces[0].shape
    rows = rows // 4
    return pl.pallas_call(
        numer_kernel,
        out_shape=jax.ShapeDtypeStruct((16, rows, columns), jnp.float32),
        in_specs=[pl.BlockSpec(memory_space=pltpu.SMEM)]
        + [pl.BlockSpec(memory_space=pltpu.VMEM)] * 4,
        out_specs=pl.BlockSpec(memory_space=pltpu.VMEM),
        compiler_params=pltpu.CompilerParams(vmem_limit_bytes=VMEM),
    )(place, *pieces)


def sums_kernel(place_ref, *refs):
    out_ref = refs[8]
    for gram in range(2):
        for slot in range(4):
            value = refs[gram * 4 + slot][...].astype(jnp.float32)
            rows = value.shape[0] // 4
            row = jnp.concatenate(
                [value[at * rows : (at + 1) * rows] for at in range(4)], axis=1
            )
            chunk = row.shape[1]
            start = pl.multiple_of((place_ref[2] ^ slot) * chunk, 128)
            out_ref[gram, :, pl.ds(start, chunk)] = row


def place_sums(place, pieces):
    rows, share = pieces[0].shape
    return pl.pallas_call(
        sums_kernel,
        out_shape=jax.ShapeDtypeStruct((2, rows // 4, 16 * share), jnp.float32),
        in_specs=[pl.BlockSpec(memory_space=pltpu.SMEM)]
        + [pl.BlockSpec(memory_space=pltpu.VMEM)] * 8,
        out_specs=pl.BlockSpec(memory_space=pltpu.VMEM),
        compiler_params=pltpu.CompilerParams(vmem_limit_bytes=VMEM),
    )(place, *pieces)


def solution(mesh):
    placed = (
        P("mp", "tok"),
        P("mp", "tok", None),
        P("mp", "tok", None),
        P("mp", None, None),
        P("mp", "col", "tok"),
        P("mp", "col", "tok"),
    )
    return jax.shard_map(
        body,
        mesh=mesh,
        in_specs=placed,
        out_specs=(
            P(None, "mp", "tok", "col", None, None),
            P("mp", None, "col", None, "tok"),
            P("mp", None, "col", None, "tok"),
        ),
        check_vma=False,
    )
```

```python
import functools

import jax
import jax.numpy as jnp
from jax import lax
from jax.experimental import pallas as pl
from jax.experimental.pallas import tpu as pltpu
from jax.sharding import PartitionSpec as P

PAD_ID = 151643
SLOTS = (0, 1, 3, 2)
VMEM = 30 * 1024 * 1024


def swap(value, axis, code):
    size = lax.axis_size(axis)
    return lax.ppermute(value, axis, [(i, i ^ code) for i in range(size)])


def total(*terms):
    out = terms[0].astype(jnp.float32)
    for term in terms[1:]:
        out = out + term.astype(jnp.float32)
    return out


def rounded(*terms, then=()):
    return (total(*terms) + nothing(*then)).astype(jnp.bfloat16)


def nothing(*values):
    zero = jnp.zeros((), jnp.float32)
    for value in values:
        zero = zero + value[(0,) * value.ndim].astype(jnp.float32) * 0.0
    return zero


def later(value, lead):
    return jnp.pad(value.astype(jnp.float32), ((lead, 0),) + ((0, 0),) * (value.ndim - 1))


def earlier(value, trail):
    return jnp.pad(value.astype(jnp.float32), ((0, trail),) + ((0, 0),) * (value.ndim - 1))


def pair(values, axis, codes):
    return tuple(swap(value, axis, code) for value, code in zip(values, codes))


class Order:
    def __init__(self, token):
        self.token = token

    def hold(self, *values):
        self.token, *out = lax.optimization_barrier((self.token, *values))
        return tuple(out)


def product_kernel(place_ref, *refs, first, columns, n_col):
    rows, weights, outs, (left_ref, right_ref) = refs[:5], refs[5:9], refs[9:14], refs[14:]
    piece, depth = rows[0].shape[1:]
    pad = left_ref.shape[0] // 4
    block = piece // n_col
    wide = 4 * columns
    share = depth // 4
    for at in range(4):
        right_ref[at * columns : (at + 1) * columns, :] = weights[at][
            first : first + columns, :
        ]
    left_ref[...] = jnp.zeros_like(left_ref)
    for slot in (2, 1, 3, 0):
        position = SLOTS.index(slot)
        for at in range(3):
            left_ref[at * pad : at * pad + piece, :] = rows[at][position]
        left_ref[3 * pad : 3 * pad + piece, :] = rows[3 + position // 2][position % 2]
        term = lax.dot_general(
            left_ref[...],
            right_ref[...],
            (((1,), (1,)), ((), ())),
            preferred_element_type=jnp.float32,
        )
        own = rows[0][position].astype(jnp.float32)
        for col in range(n_col):
            held = place_ref[2] ^ col
            if slot == 2:
                out_ref, index = None, held
            else:
                out_ref, index = outs[2 + (1, 3, 0).index(slot)], held
            start = col * block
            product = jnp.concatenate(
                [term[at * pad + start : at * pad + start + block] for at in range(4)], axis=0
            ).astype(jnp.bfloat16)
            gram = jnp.concatenate(
                [
                    own[start : start + block, at * share : (at + 1) * share]
                    for at in range(4)
                ],
                axis=0,
            ).astype(jnp.bfloat16)
            if slot == 2:
                for half in range(2):

                    @pl.when(index // 2 == half)
                    def _(half=half, product=product, gram=gram, index=index):
                        outs[half][index % 2, :, :wide] = product
                        outs[half][index % 2, :, wide:] = gram

            else:
                out_ref[index, :, :wide] = product
                out_ref[index, :, wide:] = gram


def products(place, rows, weights, first, columns, n_col):
    piece, depth = rows[0].shape[1:]
    wide = 4 * columns
    half = jax.ShapeDtypeStruct((2, piece, wide + depth // 4), jnp.bfloat16)
    whole = jax.ShapeDtypeStruct((4, piece, wide + depth // 4), jnp.bfloat16)
    pad = -(-piece // 16) * 16
    return pl.pallas_call(
        functools.partial(product_kernel, first=first, columns=columns, n_col=n_col),
        out_shape=[half, half, whole, whole, whole],
        in_specs=[pl.BlockSpec(memory_space=pltpu.SMEM)]
        + [pl.BlockSpec(memory_space=pltpu.VMEM)] * 9,
        out_specs=[pl.BlockSpec(memory_space=pltpu.VMEM)] * 5,
        scratch_shapes=[
            pltpu.VMEM((4 * pad, depth), jnp.bfloat16),
            pltpu.VMEM((wide, depth), jnp.bfloat16),
        ],
        compiler_params=pltpu.CompilerParams(vmem_limit_bytes=VMEM),
        cost_estimate=pl.CostEstimate(
            flops=2 * 16 * pad * depth * wide, bytes_accessed=12 * 2**20, transcendentals=0
        ),
    )(place, *rows, *weights)


def last_of(one, three, far, then=()):
    half = far[0].shape[0]
    return (
        rounded(one, later(far[1], half), then=then),
        rounded(three, earlier(far[0], half), then=then),
    )


def ring_all(value, axis, codes):
    half = value.shape[0] // 2
    near = pair((value, value), axis, codes)
    return (*near, *pair((near[1][:half], near[0][half:]), axis, codes))


def col_last(one, three, far):
    lead, trail = far[0].shape[0], far[1].shape[0]
    rest = (0, one.shape[1] - far[0].shape[1])
    far = [value.astype(jnp.float32) for value in far]
    return (
        rounded(one, jnp.pad(far[1], ((lead, 0), rest))),
        rounded(three, jnp.pad(far[0], ((0, trail), rest))),
    )


def column_blocks(home, got, wide):
    value = rounded(*[term[:, :wide] for term in (home, *got)])
    each = wide // 4
    return [value[:, slot * each : (slot + 1) * each] for slot in range(4)]


def body(ids, hidden_in, hidden_mid, norm_gains, q_weight, gate_weight):
    n_mp = lax.axis_size("mp")
    n_tok = lax.axis_size("tok")
    n_col = lax.axis_size("col")
    col_index = lax.axis_index("col")
    width = hidden_in.shape[2]
    row_block = width // (n_mp * n_tok * n_col)
    piece = row_block * n_col
    place = jnp.stack([lax.axis_index("mp"), lax.axis_index("tok"), col_index]).astype(jnp.int32)
    y_codes, ring_codes = (4, 12), (1, 3)
    order = Order(place)
    hold = order.hold
    n_gate, n_query = gate_weight.shape[2], q_weight.shape[2]

    def core_parts(keep, got):
        return {slot: (keep[at], got[at]) for at, slot in enumerate(SLOTS)}

    def y_far(parts):
        return (
            rounded(*[term[:1] for term in parts[2]]),
            rounded(*[term[1:] for term in parts[2]]),
        )

    def y_last(parts, far, then=()):
        return (
            rounded(*parts[1], later(far[1], 1), then=then),
            rounded(*parts[3], earlier(far[0], 1), then=then),
        )

    def away_rows(parts, last):
        return rounded(*[term[1] for term in (*parts[0], *last)])

    def home_rows(parts, last, got, then=()):
        home = total(*[term[0] for term in (*parts[0], *last)], got) + nothing(*then)
        return (home / count[0, 0]).astype(jnp.bfloat16)

    weight = jnp.concatenate([gate_weight[0].T, q_weight[0].T], axis=0)
    weight_far = swap(weight, "tok", 2)
    gate_keep, gate_send, count = hold(
        *gram_parts(place, hidden_mid, ids, norm_gains, 1, n_mp, piece)
    )
    gate_got = swap(gate_send, "tok", 1)
    query_place = place + (count[0, :3] * 0.0).astype(jnp.int32)
    query_keep, query_send, _ = hold(
        *gram_parts(query_place, hidden_in, ids, norm_gains, 0, n_mp, piece)
    )
    (gate_got,) = hold(gate_got)
    gate_parts = core_parts(gate_keep, gate_got)
    far = hold(*y_far(gate_parts))
    gate_far = pair(far, "tok", y_codes)
    count_got = swap(count, "tok", 4)
    query_got = swap(query_send, "tok", 1)
    (query_got,) = hold(query_got)
    query_parts = core_parts(query_keep, query_got)
    early = hold(*y_far(query_parts))
    *gate_far, count_got = hold(*gate_far, count_got)
    *last, count = hold(*y_last(gate_parts, gate_far), count + count_got)
    gate_last = pair(last, "tok", y_codes)
    weight_near = swap(weight, "tok", 1)
    count = count + swap(count, "tok", 1)
    count_got = swap(count, "tok", 12)
    *gate_last, count_got = hold(*gate_last, count_got)
    away, count, *early = hold(away_rows(gate_parts, gate_last), count + count_got, *early)
    gate_got = swap(away, "tok", 2)
    count_got = swap(count, "tok", 2)
    weight_far = rounded(weight_far, then=(away,))
    weights = [weight, weight_near, weight_far, swap(weight_far, "tok", 1)]
    query_far = pair(early, "tok", y_codes)
    gate_got, count_got = hold(gate_got, count_got)
    count = count + count_got
    query_far = hold(*query_far)
    gate_own, count = hold(home_rows(gate_parts, gate_last, gate_got, query_far[1:]), count)
    gate_ring = ring_all(gate_own, "tok", y_codes)
    gate_ring = hold(*gate_ring)
    last = hold(*y_last(query_parts, query_far, gate_ring[3:]))
    query_last = pair(last, "tok", y_codes)
    far_a, far_b, one, three, gate_home = hold(
        *products(place, (gate_own, *gate_ring), weights, 0, n_gate, n_col)
    )
    gate_far = pair((far_a, far_b), "mp", ring_codes)
    gate_far = hold(*gate_far)
    last = hold(*last_of(one, three, gate_far))
    gate_last = pair(last, "mp", ring_codes)
    query_last = hold(*query_last)
    (away,) = hold(away_rows(query_parts, query_last))
    query_got = swap(away, "tok", 2)
    (query_got,) = hold(query_got)
    (query_own,) = hold(home_rows(query_parts, query_last, query_got, last[1:]))
    query_ring = ring_all(query_own, "tok", y_codes)
    gate_last = hold(*gate_last)
    gate_home, *parts = hold(*[rounded(*[v[at] for v in (gate_home, *gate_last)]) for at in range(4)])
    gate_zh = parts
    late_place = place + nothing(parts[0]).astype(jnp.int32)
    gate_got = [swap(parts[slot - 1], "col", slot) for slot in (2, 1, 3)]
    query_ring = hold(*query_ring)
    far_a, far_b, one, three, query_home = hold(
        *products(late_place, (query_own, *query_ring), weights, n_gate, n_query, n_col)
    )
    query_far = pair((far_a, far_b), "mp", ring_codes)
    query_far = hold(*query_far)
    last = hold(*last_of(one, three, query_far))
    query_last = pair(last, "mp", ring_codes)
    query_last = hold(*query_last)
    query_home, *parts = hold(*[rounded(*[v[at] for v in (query_home, *query_last)]) for at in range(4)])
    split, wide = 24, 4 * n_query
    far = (parts[1][:split, :wide], parts[1][split:, :wide])
    query_far = pair(far, "col", ring_codes)
    query_far = hold(*query_far)
    last = hold(*col_last(parts[0], parts[2], query_far))
    query_got = pair(last, "col", ring_codes)
    query_across = swap(parts[1][:, wide:], "col", 2)
    gate_got = hold(*gate_got)
    parts = hold(*column_blocks(gate_home, gate_got, 4 * n_gate))
    gate_pieces = [parts[0]] + [swap(parts[slot], "tok", slot) for slot in (1, 2, 3)]
    query_got = hold(*query_got)
    parts = hold(*column_blocks(query_home, query_got, wide))
    query_pieces = [parts[0]] + [swap(parts[slot], "tok", slot) for slot in (1, 2, 3)]
    gate_pieces = hold(*gate_pieces)
    (gate_numer,) = hold(place_numer(place, gate_pieces))
    sum_pieces = [query_home[:, wide:], query_got[0][:, wide:]]
    sum_pieces += [query_across, query_got[1][:, wide:]]
    sum_pieces += [value[:, 4 * n_gate :] for value in (gate_home, *gate_got)]
    sum_pieces = [sum_pieces[at] for at in (0, 1, 2, 3, 4, 6, 5, 7)]
    (gram_sums,) = hold(place_sums(place, sum_pieces))
    query_pieces = hold(*query_pieces)
    query_numer = place_numer(place, query_pieces)
    return (
        gram_sums[:, None, None, None],
        query_numer[None, :, None],
        gate_numer[None, :, None],
    )


def gram_kernel(place_ref, hidden_ref, ids_ref, gain_ref, *rest, piece, gain_row):
    (keep_ref, send_ref, count_ref), (scale_ref, right_ref, acc_ref) = rest[:3], rest[3:]
    step = pl.program_id(0)
    width = hidden_ref.shape[2]
    chunk = right_ref.shape[1]
    tok = place_ref[1]

    def normed(start):
        start = pl.multiple_of(start, 128)
        values = hidden_ref[0, :, pl.ds(start, chunk)].astype(jnp.float32)
        gain = gain_ref[0, gain_row : gain_row + 1, pl.ds(start, chunk)]
        return (values * scale_ref[...] * gain).astype(jnp.bfloat16)

    @pl.when(step == 0)
    def _():
        squares = jnp.zeros((hidden_ref.shape[1], 128), jnp.float32)
        for lane in range(0, width, 128):
            values = hidden_ref[0, :, lane : lane + 128].astype(jnp.float32)
            squares = squares + values * values
        mean = jnp.sum(squares, axis=1, keepdims=True) / width
        live = (ids_ref[...] != PAD_ID).astype(jnp.float32)
        count_ref[...] = jnp.full(count_ref.shape, jnp.sum(live))
        live = jnp.broadcast_to(live, (128, live.shape[1])).T[:, :1]
        scale_ref[...] = lax.rsqrt(mean + 1e-06) * live
        right_ref[...] = normed(place_ref[2] * chunk)

    slot = jnp.where(step == 0, 0, jnp.where(step == 1, 1, jnp.where(step == 2, 3, 2)))
    left = normed((place_ref[0] ^ slot) * chunk)
    acc_ref[...] = lax.dot_general(
        left, right_ref[...], (((0,), (0,)), ((), ())), preferred_element_type=jnp.float32
    )
    for core, out_ref in enumerate((keep_ref, send_ref)):
        for at, y_slot in enumerate(SLOTS):
            for z_slot in range(2):
                source = (tok ^ (y_slot * 4 + z_slot * 2 + core)) * piece
                rows = acc_ref[pl.ds(pl.multiple_of(source, 8), piece), :]
                out_ref[at, z_slot, 0] = rows.astype(jnp.bfloat16)


def gram_parts(place, hidden, ids, gain, gain_row, n_mp, piece):
    tokens, width = hidden.shape[1:]
    chunk = width // n_mp
    out = jax.ShapeDtypeStruct((4, 2, n_mp, piece, chunk), jnp.bfloat16)
    return pl.pallas_call(
        functools.partial(gram_kernel, piece=piece, gain_row=gain_row),
        out_shape=[out, out, jax.ShapeDtypeStruct((8, 128), jnp.float32)],
        grid_spec=pltpu.PrefetchScalarGridSpec(
            num_scalar_prefetch=1,
            grid=(n_mp,),
            in_specs=[
                pl.BlockSpec((1, tokens, width), lambda i, place: (0, 0, 0)),
                pl.BlockSpec((1, tokens), lambda i, place: (0, 0)),
                pl.BlockSpec((1, 2, width), lambda i, place: (0, 0, 0)),
            ],
            out_specs=[
                pl.BlockSpec((4, 2, 1, piece, chunk), lambda i, place: (0, 0, i, 0, 0))
            ]
            * 2
            + [pl.BlockSpec((8, 128), lambda i, place: (0, 0))],
            scratch_shapes=[
                pltpu.VMEM((tokens, 1), jnp.float32),
                pltpu.VMEM((tokens, chunk), jnp.bfloat16),
                pltpu.VMEM((chunk, chunk), jnp.float32),
            ],
        ),
        compiler_params=pltpu.CompilerParams(vmem_limit_bytes=VMEM),
        cost_estimate=pl.CostEstimate(
            flops=2 * tokens * width * chunk, bytes_accessed=10 * 2**20, transcendentals=tokens
        ),
    )(place, hidden, ids, gain)


def numer_kernel(place_ref, *refs):
    out_ref = refs[4]
    rows = out_ref.shape[1]
    for q_slot in range(4):
        value = refs[q_slot][...].astype(jnp.float32)
        for at, y_slot in enumerate(SLOTS):
            out_ref[place_ref[1] ^ (y_slot * 4 + q_slot)] = value[at * rows : (at + 1) * rows]


def place_numer(place, pieces):
    rows, columns = pieces[0].shape
    rows = rows // 4
    return pl.pallas_call(
        numer_kernel,
        out_shape=jax.ShapeDtypeStruct((16, rows, columns), jnp.float32),
        in_specs=[pl.BlockSpec(memory_space=pltpu.SMEM)]
        + [pl.BlockSpec(memory_space=pltpu.VMEM)] * 4,
        out_specs=pl.BlockSpec(memory_space=pltpu.VMEM),
        compiler_params=pltpu.CompilerParams(vmem_limit_bytes=VMEM),
    )(place, *pieces)


def sums_kernel(place_ref, *refs):
    out_ref = refs[8]
    for gram in range(2):
        for slot in range(4):
            value = refs[gram * 4 + slot][...].astype(jnp.float32)
            rows = value.shape[0] // 4
            row = jnp.concatenate(
                [value[at * rows : (at + 1) * rows] for at in range(4)], axis=1
            )
            chunk = row.shape[1]
            start = pl.multiple_of((place_ref[2] ^ slot) * chunk, 128)
            out_ref[gram, :, pl.ds(start, chunk)] = row


def place_sums(place, pieces):
    rows, share = pieces[0].shape
    return pl.pallas_call(
        sums_kernel,
        out_shape=jax.ShapeDtypeStruct((2, rows // 4, 16 * share), jnp.float32),
        in_specs=[pl.BlockSpec(memory_space=pltpu.SMEM)]
        + [pl.BlockSpec(memory_space=pltpu.VMEM)] * 8,
        out_specs=pl.BlockSpec(memory_space=pltpu.VMEM),
        compiler_params=pltpu.CompilerParams(vmem_limit_bytes=VMEM),
    )(place, *pieces)


def solution(mesh):
    placed = (
        P("mp", "tok"),
        P("mp", "tok", None),
        P("mp", "tok", None),
        P("mp", None, None),
        P("mp", "col", "tok"),
        P("mp", "col", "tok"),
    )
    return jax.shard_map(
        body,
        mesh=mesh,
        in_specs=placed,
        out_specs=(
            P(None, "mp", "tok", "col", None, None),
            P("mp", None, "col", None, "tok"),
            P("mp", None, "col", None, "tok"),
        ),
        check_vma=False,
    )
```

```python
import functools

import jax
import jax.numpy as jnp
from jax import lax
from jax.experimental import pallas as pl
from jax.experimental.pallas import tpu as pltpu
from jax.sharding import PartitionSpec as P

PAD_ID = 151643
SLOTS = (0, 1, 3, 2)
VMEM = 30 * 1024 * 1024


def swap(value, axis, code):
    size = lax.axis_size(axis)
    return lax.ppermute(value, axis, [(i, i ^ code) for i in range(size)])


def total(*terms):
    out = terms[0].astype(jnp.float32)
    for term in terms[1:]:
        out = out + term.astype(jnp.float32)
    return out


def rounded(*terms, then=()):
    return (total(*terms) + nothing(*then)).astype(jnp.bfloat16)


def nothing(*values):
    zero = jnp.zeros((), jnp.float32)
    for value in values:
        zero = zero + value[(0,) * value.ndim].astype(jnp.float32) * 0.0
    return zero


def later(value, lead):
    return jnp.pad(value.astype(jnp.float32), ((lead, 0),) + ((0, 0),) * (value.ndim - 1))


def earlier(value, trail):
    return jnp.pad(value.astype(jnp.float32), ((0, trail),) + ((0, 0),) * (value.ndim - 1))


def pair(values, axis, codes):
    return tuple(swap(value, axis, code) for value, code in zip(values, codes))


class Order:
    def __init__(self, token):
        self.token = token

    def hold(self, *values):
        self.token, *out = lax.optimization_barrier((self.token, *values))
        return tuple(out)


def product_kernel(place_ref, *refs, first, columns, n_col):
    rows, weights, outs, (left_ref, right_ref) = refs[:5], refs[5:9], refs[9:14], refs[14:]
    piece, depth = rows[0].shape[1:]
    pad = left_ref.shape[0] // 4
    block = piece // n_col
    wide = 4 * columns
    share = depth // 4
    for at in range(4):
        right_ref[at * columns : (at + 1) * columns, :] = weights[at][
            first : first + columns, :
        ]
    left_ref[...] = jnp.zeros_like(left_ref)
    for slot in (2, 1, 3, 0):
        position = SLOTS.index(slot)
        for at in range(3):
            left_ref[at * pad : at * pad + piece, :] = rows[at][position]
        left_ref[3 * pad : 3 * pad + piece, :] = rows[3 + position // 2][position % 2]
        term = lax.dot_general(
            left_ref[...],
            right_ref[...],
            (((1,), (1,)), ((), ())),
            preferred_element_type=jnp.float32,
        )
        own = rows[0][position].astype(jnp.float32)
        for col in range(n_col):
            held = place_ref[2] ^ col
            if slot == 2:
                out_ref, index = None, held
            else:
                out_ref, index = outs[2 + (1, 3, 0).index(slot)], held
            start = col * block
            product = jnp.concatenate(
                [term[at * pad + start : at * pad + start + block] for at in range(4)], axis=0
            ).astype(jnp.bfloat16)
            gram = jnp.concatenate(
                [
                    own[start : start + block, at * share : (at + 1) * share]
                    for at in range(4)
                ],
                axis=0,
            ).astype(jnp.bfloat16)
            if slot == 2:
                for half in range(2):

                    @pl.when(index // 2 == half)
                    def _(half=half, product=product, gram=gram, index=index):
                        outs[half][index % 2, :, :wide] = product
                        outs[half][index % 2, :, wide:] = gram

            else:
                out_ref[index, :, :wide] = product
                out_ref[index, :, wide:] = gram


def products(place, rows, weights, first, columns, n_col):
    piece, depth = rows[0].shape[1:]
    wide = 4 * columns
    half = jax.ShapeDtypeStruct((2, piece, wide + depth // 4), jnp.bfloat16)
    whole = jax.ShapeDtypeStruct((4, piece, wide + depth // 4), jnp.bfloat16)
    pad = -(-piece // 16) * 16
    return pl.pallas_call(
        functools.partial(product_kernel, first=first, columns=columns, n_col=n_col),
        out_shape=[half, half, whole, whole, whole],
        in_specs=[pl.BlockSpec(memory_space=pltpu.SMEM)]
        + [pl.BlockSpec(memory_space=pltpu.VMEM)] * 9,
        out_specs=[pl.BlockSpec(memory_space=pltpu.VMEM)] * 5,
        scratch_shapes=[
            pltpu.VMEM((4 * pad, depth), jnp.bfloat16),
            pltpu.VMEM((wide, depth), jnp.bfloat16),
        ],
        compiler_params=pltpu.CompilerParams(vmem_limit_bytes=VMEM),
        cost_estimate=pl.CostEstimate(
            flops=2 * 16 * pad * depth * wide, bytes_accessed=12 * 2**20, transcendentals=0
        ),
    )(place, *rows, *weights)


def last_of(one, three, far, then=()):
    half = far[0].shape[0]
    return (
        rounded(one, later(far[1], half), then=then),
        rounded(three, earlier(far[0], half), then=then),
    )


def ring_all(value, axis, codes):
    half = value.shape[0] // 2
    near = pair((value, value), axis, codes)
    return (*near, *pair((near[1][:half], near[0][half:]), axis, codes))


def col_last(one, three, far):
    lead, trail = far[0].shape[0], far[1].shape[0]
    rest = (0, one.shape[1] - far[0].shape[1])
    far = [value.astype(jnp.float32) for value in far]
    return (
        rounded(one, jnp.pad(far[1], ((lead, 0), rest))),
        rounded(three, jnp.pad(far[0], ((0, trail), rest))),
    )


def column_blocks(home, got, wide):
    value = rounded(*[term[:, :wide] for term in (home, *got)])
    each = wide // 4
    return [value[:, slot * each : (slot + 1) * each] for slot in range(4)]


def body(ids, hidden_in, hidden_mid, norm_gains, q_weight, gate_weight):
    n_mp = lax.axis_size("mp")
    n_tok = lax.axis_size("tok")
    n_col = lax.axis_size("col")
    col_index = lax.axis_index("col")
    width = hidden_in.shape[2]
    row_block = width // (n_mp * n_tok * n_col)
    piece = row_block * n_col
    place = jnp.stack([lax.axis_index("mp"), lax.axis_index("tok"), col_index]).astype(jnp.int32)
    y_codes, ring_codes = (4, 12), (1, 3)
    order = Order(place)
    hold = order.hold
    n_gate, n_query = gate_weight.shape[2], q_weight.shape[2]

    def core_parts(keep, got):
        return {slot: (keep[at], got[at]) for at, slot in enumerate(SLOTS)}

    def y_far(parts):
        return (
            rounded(*[term[:1] for term in parts[2]]),
            rounded(*[term[1:] for term in parts[2]]),
        )

    def y_last(parts, far, then=()):
        return (
            rounded(*parts[1], later(far[1], 1), then=then),
            rounded(*parts[3], earlier(far[0], 1), then=then),
        )

    def away_rows(parts, last):
        return rounded(*[term[1] for term in (*parts[0], *last)])

    def home_rows(parts, last, got, then=()):
        home = total(*[term[0] for term in (*parts[0], *last)], got) + nothing(*then)
        return (home / count[0, 0]).astype(jnp.bfloat16)

    weight = jnp.concatenate([gate_weight[0].T, q_weight[0].T], axis=0)
    weight_far = swap(weight, "tok", 2)
    gate_keep, gate_send, count = hold(
        *gram_parts(place, hidden_mid, ids, norm_gains, 1, n_mp, piece)
    )
    gate_got = swap(gate_send, "tok", 1)
    query_place = place + (count[0, :3] * 0.0).astype(jnp.int32)
    query_keep, query_send, _ = hold(
        *gram_parts(query_place, hidden_in, ids, norm_gains, 0, n_mp, piece)
    )
    (gate_got,) = hold(gate_got)
    gate_parts = core_parts(gate_keep, gate_got)
    far = hold(*y_far(gate_parts))
    gate_far = pair(far, "tok", y_codes)
    count_got = swap(count, "tok", 4)
    query_got = swap(query_send, "tok", 1)
    (query_got,) = hold(query_got)
    query_parts = core_parts(query_keep, query_got)
    early = hold(*y_far(query_parts))
    *gate_far, count_got = hold(*gate_far, count_got)
    *last, count = hold(*y_last(gate_parts, gate_far), count + count_got)
    gate_last = pair(last, "tok", y_codes)
    weight_near = swap(weight, "tok", 1)
    count = count + swap(count, "tok", 1)
    count_got = swap(count, "tok", 12)
    *gate_last, count_got = hold(*gate_last, count_got)
    away, count, *early = hold(away_rows(gate_parts, gate_last), count + count_got, *early)
    gate_got = swap(away, "tok", 2)
    count_got = swap(count, "tok", 2)
    weight_far = rounded(weight_far, then=(away,))
    weights = [weight, weight_near, weight_far, swap(weight_far, "tok", 1)]
    query_far = pair(early, "tok", y_codes)
    gate_got, count_got = hold(gate_got, count_got)
    count = count + count_got
    query_far = hold(*query_far)
    gate_own, count = hold(home_rows(gate_parts, gate_last, gate_got, query_far[1:]), count)
    gate_ring = ring_all(gate_own, "tok", y_codes)
    gate_ring = hold(*gate_ring)
    last = hold(*y_last(query_parts, query_far, gate_ring[3:]))
    query_last = pair(last, "tok", y_codes)
    far_a, far_b, one, three, gate_home = hold(
        *products(place, (gate_own, *gate_ring), weights, 0, n_gate, n_col)
    )
    gate_far = pair((far_a, far_b), "mp", ring_codes)
    gate_far = hold(*gate_far)
    last = hold(*last_of(one, three, gate_far))
    gate_last = pair(last, "mp", ring_codes)
    query_last = hold(*query_last)
    (away,) = hold(away_rows(query_parts, query_last))
    query_got = swap(away, "tok", 2)
    (query_got,) = hold(query_got)
    (query_own,) = hold(home_rows(query_parts, query_last, query_got, last[1:]))
    query_ring = ring_all(query_own, "tok", y_codes)
    gate_last = hold(*gate_last)
    gate_home, *parts = hold(*[rounded(*[v[at] for v in (gate_home, *gate_last)]) for at in range(4)])
    gate_zh = parts
    late_place = place + nothing(parts[0]).astype(jnp.int32)
    split, wide = 24, 4 * n_gate
    far = (parts[1][:split, :wide], parts[1][split:, :wide])
    gate_far = pair(far, "col", ring_codes)
    query_ring = hold(*query_ring)
    far_a, far_b, one, three, query_home = hold(
        *products(late_place, (query_own, *query_ring), weights, n_gate, n_query, n_col)
    )
    query_far = pair((far_a, far_b), "mp", ring_codes)
    query_far = hold(*query_far)
    last = hold(*last_of(one, three, query_far, gate_far[1:]))
    query_last = pair(last, "mp", ring_codes)
    gate_last = hold(*col_last(gate_zh[0], gate_zh[2], gate_far))
    gate_got = pair(gate_last, "col", ring_codes)
    query_last = hold(*query_last)
    query_home, *parts = hold(*[rounded(*[v[at] for v in (query_home, *query_last)], then=gate_got[1:]) for at in range(4)])
    wide = 4 * n_query
    far = (parts[1][:split, :wide], parts[1][split:, :wide])
    query_far = pair(far, "col", ring_codes)
    query_far = hold(*query_far)
    last = hold(*col_last(parts[0], parts[2], query_far))
    query_got = pair(last, "col", ring_codes)
    across = (parts[1][:, wide:], gate_zh[1][:, 4 * n_gate :])
    across = swap(jnp.concatenate(across, axis=0), "col", 2)
    gate_got = hold(*gate_got)
    parts = hold(*column_blocks(gate_home, gate_got, 4 * n_gate))
    gate_pieces = [parts[0]] + [swap(parts[slot], "tok", slot) for slot in (1, 2, 3)]
    query_got = hold(*query_got)
    parts = hold(*column_blocks(query_home, query_got, wide))
    query_pieces = [parts[0]] + [swap(parts[slot], "tok", slot) for slot in (1, 2, 3)]
    gate_pieces = hold(*gate_pieces)
    (gate_numer,) = hold(place_numer(place, gate_pieces))
    sum_pieces = [
        query_home[:, wide:],
        query_got[0][:, wide:],
        across[:piece],
        query_got[1][:, wide:],
    ]
    wide = 4 * n_gate
    sum_pieces += [
        gate_home[:, wide:],
        gate_got[0][:, wide:],
        across[piece:],
        gate_got[1][:, wide:],
    ]
    (gram_sums,) = hold(place_sums(place, sum_pieces))
    query_pieces = hold(*query_pieces)
    query_numer = place_numer(place, query_pieces)
    return (
        gram_sums[:, None, None, None],
        query_numer[None, :, None],
        gate_numer[None, :, None],
    )


def gram_kernel(place_ref, hidden_ref, ids_ref, gain_ref, *rest, piece, gain_row):
    (keep_ref, send_ref, count_ref), (scale_ref, right_ref, acc_ref) = rest[:3], rest[3:]
    step = pl.program_id(0)
    width = hidden_ref.shape[2]
    chunk = right_ref.shape[1]
    tok = place_ref[1]

    def normed(start):
        start = pl.multiple_of(start, 128)
        values = hidden_ref[0, :, pl.ds(start, chunk)].astype(jnp.float32)
        gain = gain_ref[0, gain_row : gain_row + 1, pl.ds(start, chunk)]
        return (values * scale_ref[...] * gain).astype(jnp.bfloat16)

    @pl.when(step == 0)
    def _():
        squares = jnp.zeros((hidden_ref.shape[1], 128), jnp.float32)
        for lane in range(0, width, 128):
            values = hidden_ref[0, :, lane : lane + 128].astype(jnp.float32)
            squares = squares + values * values
        mean = jnp.sum(squares, axis=1, keepdims=True) / width
        live = (ids_ref[...] != PAD_ID).astype(jnp.float32)
        count_ref[...] = jnp.full(count_ref.shape, jnp.sum(live))
        live = jnp.broadcast_to(live, (128, live.shape[1])).T[:, :1]
        scale_ref[...] = lax.rsqrt(mean + 1e-06) * live
        right_ref[...] = normed(place_ref[2] * chunk)

    slot = jnp.where(step == 0, 0, jnp.where(step == 1, 1, jnp.where(step == 2, 3, 2)))
    left = normed((place_ref[0] ^ slot) * chunk)
    acc_ref[...] = lax.dot_general(
        left, right_ref[...], (((0,), (0,)), ((), ())), preferred_element_type=jnp.float32
    )
    for core, out_ref in enumerate((keep_ref, send_ref)):
        for at, y_slot in enumerate(SLOTS):
            for z_slot in range(2):
                source = (tok ^ (y_slot * 4 + z_slot * 2 + core)) * piece
                rows = acc_ref[pl.ds(pl.multiple_of(source, 8), piece), :]
                out_ref[at, z_slot, 0] = rows.astype(jnp.bfloat16)


def gram_parts(place, hidden, ids, gain, gain_row, n_mp, piece):
    tokens, width = hidden.shape[1:]
    chunk = width // n_mp
    out = jax.ShapeDtypeStruct((4, 2, n_mp, piece, chunk), jnp.bfloat16)
    return pl.pallas_call(
        functools.partial(gram_kernel, piece=piece, gain_row=gain_row),
        out_shape=[out, out, jax.ShapeDtypeStruct((8, 128), jnp.float32)],
        grid_spec=pltpu.PrefetchScalarGridSpec(
            num_scalar_prefetch=1,
            grid=(n_mp,),
            in_specs=[
                pl.BlockSpec((1, tokens, width), lambda i, place: (0, 0, 0)),
                pl.BlockSpec((1, tokens), lambda i, place: (0, 0)),
                pl.BlockSpec((1, 2, width), lambda i, place: (0, 0, 0)),
            ],
            out_specs=[
                pl.BlockSpec((4, 2, 1, piece, chunk), lambda i, place: (0, 0, i, 0, 0))
            ]
            * 2
            + [pl.BlockSpec((8, 128), lambda i, place: (0, 0))],
            scratch_shapes=[
                pltpu.VMEM((tokens, 1), jnp.float32),
                pltpu.VMEM((tokens, chunk), jnp.bfloat16),
                pltpu.VMEM((chunk, chunk), jnp.float32),
            ],
        ),
        compiler_params=pltpu.CompilerParams(vmem_limit_bytes=VMEM),
        cost_estimate=pl.CostEstimate(
            flops=2 * tokens * width * chunk, bytes_accessed=10 * 2**20, transcendentals=tokens
        ),
    )(place, hidden, ids, gain)


def numer_kernel(place_ref, *refs):
    out_ref = refs[4]
    rows = out_ref.shape[1]
    for q_slot in range(4):
        value = refs[q_slot][...].astype(jnp.float32)
        for at, y_slot in enumerate(SLOTS):
            out_ref[place_ref[1] ^ (y_slot * 4 + q_slot)] = value[at * rows : (at + 1) * rows]


def place_numer(place, pieces):
    rows, columns = pieces[0].shape
    rows = rows // 4
    return pl.pallas_call(
        numer_kernel,
        out_shape=jax.ShapeDtypeStruct((16, rows, columns), jnp.float32),
        in_specs=[pl.BlockSpec(memory_space=pltpu.SMEM)]
        + [pl.BlockSpec(memory_space=pltpu.VMEM)] * 4,
        out_specs=pl.BlockSpec(memory_space=pltpu.VMEM),
        compiler_params=pltpu.CompilerParams(vmem_limit_bytes=VMEM),
    )(place, *pieces)


def sums_kernel(place_ref, *refs):
    out_ref = refs[8]
    for gram in range(2):
        for slot in range(4):
            value = refs[gram * 4 + slot][...].astype(jnp.float32)
            rows = value.shape[0] // 4
            row = jnp.concatenate(
                [value[at * rows : (at + 1) * rows] for at in range(4)], axis=1
            )
            chunk = row.shape[1]
            start = pl.multiple_of((place_ref[2] ^ slot) * chunk, 128)
            out_ref[gram, :, pl.ds(start, chunk)] = row


def place_sums(place, pieces):
    rows, share = pieces[0].shape
    return pl.pallas_call(
        sums_kernel,
        out_shape=jax.ShapeDtypeStruct((2, rows // 4, 16 * share), jnp.float32),
        in_specs=[pl.BlockSpec(memory_space=pltpu.SMEM)]
        + [pl.BlockSpec(memory_space=pltpu.VMEM)] * 8,
        out_specs=pl.BlockSpec(memory_space=pltpu.VMEM),
        compiler_params=pltpu.CompilerParams(vmem_limit_bytes=VMEM),
    )(place, *pieces)


def solution(mesh):
    placed = (
        P("mp", "tok"),
        P("mp", "tok", None),
        P("mp", "tok", None),
        P("mp", None, None),
        P("mp", "col", "tok"),
        P("mp", "col", "tok"),
    )
    return jax.shard_map(
        body,
        mesh=mesh,
        in_specs=placed,
        out_specs=(
            P(None, "mp", "tok", "col", None, None),
            P("mp", None, "col", None, "tok"),
            P("mp", None, "col", None, "tok"),
        ),
        check_vma=False,
    )
```

```python
import functools

import jax
import jax.numpy as jnp
from jax import lax
from jax.experimental import pallas as pl
from jax.experimental.pallas import tpu as pltpu
from jax.sharding import PartitionSpec as P

PAD_ID = 151643
SLOTS = (0, 1, 3, 2)
VMEM = 30 * 1024 * 1024


def swap(value, axis, code):
    size = lax.axis_size(axis)
    return lax.ppermute(value, axis, [(i, i ^ code) for i in range(size)])


def total(*terms):
    out = terms[0].astype(jnp.float32)
    for term in terms[1:]:
        out = out + term.astype(jnp.float32)
    return out


def rounded(*terms, then=()):
    return (total(*terms) + nothing(*then)).astype(jnp.bfloat16)


def nothing(*values):
    zero = jnp.zeros((), jnp.float32)
    for value in values:
        zero = zero + value[(0,) * value.ndim].astype(jnp.float32) * 0.0
    return zero


def later(value, lead):
    return jnp.pad(value.astype(jnp.float32), ((lead, 0),) + ((0, 0),) * (value.ndim - 1))


def earlier(value, trail):
    return jnp.pad(value.astype(jnp.float32), ((0, trail),) + ((0, 0),) * (value.ndim - 1))


def pair(values, axis, codes):
    return tuple(swap(value, axis, code) for value, code in zip(values, codes))


class Order:
    def __init__(self, token):
        self.token = token

    def hold(self, *values):
        self.token, *out = lax.optimization_barrier((self.token, *values))
        return tuple(out)


def product_kernel(place_ref, *refs, first, columns, n_col):
    rows, weights, outs, (left_ref, right_ref) = refs[:5], refs[5:9], refs[10:15], refs[15:]
    piece, depth = rows[0].shape[1:]
    pad = left_ref.shape[0] // 4
    block = piece // n_col
    wide = 4 * columns
    share = depth // 4
    for at in range(4):
        right_ref[at * columns : (at + 1) * columns, :] = weights[at][
            first : first + columns, :
        ]
    left_ref[...] = jnp.zeros_like(left_ref)
    for slot in (2, 1, 3, 0):
        position = SLOTS.index(slot)
        for at in range(3):
            left_ref[at * pad : at * pad + piece, :] = rows[at][position]
        left_ref[3 * pad : 3 * pad + piece, :] = rows[3 + position // 2][position % 2]
        term = lax.dot_general(
            left_ref[...],
            right_ref[...],
            (((1,), (1,)), ((), ())),
            preferred_element_type=jnp.float32,
        )
        own = rows[0][position].astype(jnp.float32)
        for col in range(n_col):
            held = place_ref[2] ^ col
            if slot == 2:
                out_ref, index = None, held
            else:
                out_ref, index = outs[2 + (1, 3, 0).index(slot)], held
            start = col * block
            product = jnp.concatenate(
                [term[at * pad + start : at * pad + start + block] for at in range(4)], axis=0
            ).astype(jnp.bfloat16)
            gram = jnp.concatenate(
                [
                    own[start : start + block, at * share : (at + 1) * share]
                    for at in range(4)
                ],
                axis=0,
            ).astype(jnp.bfloat16)
            if slot == 2:
                for half in range(2):

                    @pl.when(index // 2 == half)
                    def _(half=half, product=product, gram=gram, index=index):
                        outs[half][index % 2, :, :wide] = product
                        outs[half][index % 2, :, wide:] = gram

            else:
                out_ref[index, :, :wide] = product
                out_ref[index, :, wide:] = gram


def products(place, rows, weights, behind, first, columns, n_col):
    piece, depth = rows[0].shape[1:]
    wide = 4 * columns
    half = jax.ShapeDtypeStruct((2, piece, wide + depth // 4), jnp.bfloat16)
    whole = jax.ShapeDtypeStruct((4, piece, wide + depth // 4), jnp.bfloat16)
    pad = -(-piece // 16) * 16
    return pl.pallas_call(
        functools.partial(product_kernel, first=first, columns=columns, n_col=n_col),
        out_shape=[half, half, whole, whole, whole],
        in_specs=[pl.BlockSpec(memory_space=pltpu.SMEM)]
        + [pl.BlockSpec(memory_space=pltpu.VMEM)] * 9
        + [pl.BlockSpec(memory_space=pl.ANY)],
        out_specs=[pl.BlockSpec(memory_space=pltpu.VMEM)] * 5,
        scratch_shapes=[
            pltpu.VMEM((4 * pad, depth), jnp.bfloat16),
            pltpu.VMEM((wide, depth), jnp.bfloat16),
        ],
        compiler_params=pltpu.CompilerParams(vmem_limit_bytes=VMEM),
        cost_estimate=pl.CostEstimate(
            flops=2 * 16 * pad * depth * wide, bytes_accessed=12 * 2**20, transcendentals=0
        ),
    )(place, *rows, *weights, behind)


def last_of(one, three, far, then=()):
    half = far[0].shape[0]
    return (
        rounded(one, later(far[1], half), then=then),
        rounded(three, earlier(far[0], half), then=then),
    )


def ring_all(value, axis, codes):
    half = value.shape[0] // 2
    near = pair((value, value), axis, codes)
    return (*near, *pair((near[1][:half], near[0][half:]), axis, codes))


def col_last(one, three, far):
    lead, trail = far[0].shape[0], far[1].shape[0]
    rest = (0, one.shape[1] - far[0].shape[1])
    far = [value.astype(jnp.float32) for value in far]
    return (
        rounded(one, jnp.pad(far[1], ((lead, 0), rest))),
        rounded(three, jnp.pad(far[0], ((0, trail), rest))),
    )


def column_blocks(home, got, wide):
    value = rounded(*[term[:, :wide] for term in (home, *got)])
    each = wide // 4
    return [value[:, slot * each : (slot + 1) * each] for slot in range(4)]


def body(ids, hidden_in, hidden_mid, norm_gains, q_weight, gate_weight):
    n_mp = lax.axis_size("mp")
    n_tok = lax.axis_size("tok")
    n_col = lax.axis_size("col")
    col_index = lax.axis_index("col")
    width = hidden_in.shape[2]
    row_block = width // (n_mp * n_tok * n_col)
    piece = row_block * n_col
    place = jnp.stack([lax.axis_index("mp"), lax.axis_index("tok"), col_index]).astype(jnp.int32)
    y_codes, ring_codes = (4, 12), (1, 3)
    order = Order(place)
    hold = order.hold
    n_gate, n_query = gate_weight.shape[2], q_weight.shape[2]

    def core_parts(keep, got):
        return {slot: (keep[at], got[at]) for at, slot in enumerate(SLOTS)}

    def y_far(parts):
        return (
            rounded(*[term[:1] for term in parts[2]]),
            rounded(*[term[1:] for term in parts[2]]),
        )

    def y_last(parts, far, then=()):
        return (
            rounded(*parts[1], later(far[1], 1), then=then),
            rounded(*parts[3], earlier(far[0], 1), then=then),
        )

    def away_rows(parts, last):
        return rounded(*[term[1] for term in (*parts[0], *last)])

    def home_rows(parts, last, got, then=()):
        home = total(*[term[0] for term in (*parts[0], *last)], got) + nothing(*then)
        return (home / count[0, 0]).astype(jnp.bfloat16)

    weight = jnp.concatenate([gate_weight[0].T, q_weight[0].T], axis=0)
    weight_far = swap(weight, "tok", 2)
    gate_keep, gate_send, count = hold(
        *gram_parts(place, hidden_mid, ids, norm_gains, ids, 1, n_mp, piece)
    )
    gate_got = swap(gate_send, "tok", 1)
    query_keep, query_send, _ = hold(
        *gram_parts(place, hidden_in, ids, norm_gains, count, 0, n_mp, piece)
    )
    (gate_got,) = hold(gate_got)
    gate_parts = core_parts(gate_keep, gate_got)
    far = hold(*y_far(gate_parts))
    gate_far = pair(far, "tok", y_codes)
    count_got = swap(count, "tok", 4)
    query_got = swap(query_send, "tok", 1)
    (query_got,) = hold(query_got)
    query_parts = core_parts(query_keep, query_got)
    early = hold(*y_far(query_parts))
    *gate_far, count_got = hold(*gate_far, count_got)
    *last, count = hold(*y_last(gate_parts, gate_far), count + count_got)
    gate_last = pair(last, "tok", y_codes)
    weight_near = swap(weight, "tok", 1)
    count = count + swap(count, "tok", 1)
    count_got = swap(count, "tok", 12)
    *gate_last, count_got = hold(*gate_last, count_got)
    away, count, *early = hold(away_rows(gate_parts, gate_last), count + count_got, *early)
    gate_got = swap(away, "tok", 2)
    count_got = swap(count, "tok", 2)
    weight_far = rounded(weight_far, then=(away,))
    weights = [weight, weight_near, weight_far, swap(weight_far, "tok", 1)]
    query_far = pair(early, "tok", y_codes)
    gate_got, count_got = hold(gate_got, count_got)
    count = count + count_got
    query_far = hold(*query_far)
    gate_own, count = hold(home_rows(gate_parts, gate_last, gate_got, query_far[1:]), count)
    gate_ring = ring_all(gate_own, "tok", y_codes)
    gate_ring = hold(*gate_ring)
    last = hold(*y_last(query_parts, query_far, gate_ring[3:]))
    query_last = pair(last, "tok", y_codes)
    far_a, far_b, one, three, gate_home = hold(
        *products(place, (gate_own, *gate_ring), weights, gate_own, 0, n_gate, n_col)
    )
    gate_far = pair((far_a, far_b), "mp", ring_codes)
    gate_far = hold(*gate_far)
    last = hold(*last_of(one, three, gate_far))
    gate_last = pair(last, "mp", ring_codes)
    query_last = hold(*query_last)
    (away,) = hold(away_rows(query_parts, query_last))
    query_got = swap(away, "tok", 2)
    (query_got,) = hold(query_got)
    (query_own,) = hold(home_rows(query_parts, query_last, query_got, last[1:]))
    query_ring = ring_all(query_own, "tok", y_codes)
    gate_last = hold(*gate_last)
    gate_home, *parts = hold(*[rounded(*[v[at] for v in (gate_home, *gate_last)]) for at in range(4)])
    gate_zh = parts
    split, wide = 24, 4 * n_gate
    far = (parts[1][:split, :wide], parts[1][split:, :wide])
    gate_far = pair(far, "col", ring_codes)
    query_ring = hold(*query_ring)
    far_a, far_b, one, three, query_home = hold(
        *products(place, (query_own, *query_ring), weights, gate_zh[0], n_gate, n_query, n_col)
    )
    query_far = pair((far_a, far_b), "mp", ring_codes)
    query_far = hold(*query_far)
    last = hold(*last_of(one, three, query_far, gate_far[1:]))
    query_last = pair(last, "mp", ring_codes)
    gate_last = hold(*col_last(gate_zh[0], gate_zh[2], gate_far))
    gate_got = pair(gate_last, "col", ring_codes)
    query_last = hold(*query_last)
    query_home, *parts = hold(*[rounded(*[v[at] for v in (query_home, *query_last)], then=gate_got[1:]) for at in range(4)])
    wide = 4 * n_query
    far = (parts[1][:split, :wide], parts[1][split:, :wide])
    query_far = pair(far, "col", ring_codes)
    query_far = hold(*query_far)
    last = hold(*col_last(parts[0], parts[2], query_far))
    query_got = pair(last, "col", ring_codes)
    across = (parts[1][:, wide:], gate_zh[1][:, 4 * n_gate :])
    across = swap(jnp.concatenate(across, axis=0), "col", 2)
    gate_got = hold(*gate_got)
    parts = hold(*column_blocks(gate_home, gate_got, 4 * n_gate))
    gate_pieces = [parts[0]] + [swap(parts[slot], "tok", slot) for slot in (1, 2, 3)]
    query_got = hold(*query_got)
    parts = hold(*column_blocks(query_home, query_got, wide))
    query_pieces = [parts[0]] + [swap(parts[slot], "tok", slot) for slot in (1, 2, 3)]
    gate_pieces = hold(*gate_pieces)
    (gate_numer,) = hold(place_numer(place, gate_pieces))
    sum_pieces = [
        query_home[:, wide:],
        query_got[0][:, wide:],
        across[:piece],
        query_got[1][:, wide:],
    ]
    wide = 4 * n_gate
    sum_pieces += [
        gate_home[:, wide:],
        gate_got[0][:, wide:],
        across[piece:],
        gate_got[1][:, wide:],
    ]
    (gram_sums,) = hold(place_sums(place, sum_pieces))
    query_pieces = hold(*query_pieces)
    query_numer = place_numer(place, query_pieces)
    return (
        gram_sums[:, None, None, None],
        query_numer[None, :, None],
        gate_numer[None, :, None],
    )


def gram_kernel(place_ref, hidden_ref, ids_ref, gain_ref, _, *rest, piece, gain_row):
    (keep_ref, send_ref, count_ref), (scale_ref, right_ref, acc_ref) = rest[:3], rest[3:]
    step = pl.program_id(0)
    width = hidden_ref.shape[2]
    chunk = right_ref.shape[1]
    tok = place_ref[1]

    def normed(start):
        start = pl.multiple_of(start, 128)
        values = hidden_ref[0, :, pl.ds(start, chunk)].astype(jnp.float32)
        gain = gain_ref[0, gain_row : gain_row + 1, pl.ds(start, chunk)]
        return (values * scale_ref[...] * gain).astype(jnp.bfloat16)

    @pl.when(step == 0)
    def _():
        squares = jnp.zeros((hidden_ref.shape[1], 128), jnp.float32)
        for lane in range(0, width, 128):
            values = hidden_ref[0, :, lane : lane + 128].astype(jnp.float32)
            squares = squares + values * values
        mean = jnp.sum(squares, axis=1, keepdims=True) / width
        live = (ids_ref[...] != PAD_ID).astype(jnp.float32)
        count_ref[...] = jnp.full(count_ref.shape, jnp.sum(live))
        live = jnp.broadcast_to(live, (128, live.shape[1])).T[:, :1]
        scale_ref[...] = lax.rsqrt(mean + 1e-06) * live
        right_ref[...] = normed(place_ref[2] * chunk)

    slot = jnp.where(step == 0, 0, jnp.where(step == 1, 1, jnp.where(step == 2, 3, 2)))
    left = normed((place_ref[0] ^ slot) * chunk)
    acc_ref[...] = lax.dot_general(
        left, right_ref[...], (((0,), (0,)), ((), ())), preferred_element_type=jnp.float32
    )
    for core, out_ref in enumerate((keep_ref, send_ref)):
        for at, y_slot in enumerate(SLOTS):
            for z_slot in range(2):
                source = (tok ^ (y_slot * 4 + z_slot * 2 + core)) * piece
                rows = acc_ref[pl.ds(pl.multiple_of(source, 8), piece), :]
                out_ref[at, z_slot, 0] = rows.astype(jnp.bfloat16)


def gram_parts(place, hidden, ids, gain, behind, gain_row, n_mp, piece):
    tokens, width = hidden.shape[1:]
    chunk = width // n_mp
    out = jax.ShapeDtypeStruct((4, 2, n_mp, piece, chunk), jnp.bfloat16)
    return pl.pallas_call(
        functools.partial(gram_kernel, piece=piece, gain_row=gain_row),
        out_shape=[out, out, jax.ShapeDtypeStruct((8, 128), jnp.float32)],
        grid_spec=pltpu.PrefetchScalarGridSpec(
            num_scalar_prefetch=1,
            grid=(n_mp,),
            in_specs=[
                pl.BlockSpec((1, tokens, width), lambda i, place: (0, 0, 0)),
                pl.BlockSpec((1, tokens), lambda i, place: (0, 0)),
                pl.BlockSpec((1, 2, width), lambda i, place: (0, 0, 0)),
                pl.BlockSpec(memory_space=pl.ANY),
            ],
            out_specs=[
                pl.BlockSpec((4, 2, 1, piece, chunk), lambda i, place: (0, 0, i, 0, 0))
            ]
            * 2
            + [pl.BlockSpec((8, 128), lambda i, place: (0, 0))],
            scratch_shapes=[
                pltpu.VMEM((tokens, 1), jnp.float32),
                pltpu.VMEM((tokens, chunk), jnp.bfloat16),
                pltpu.VMEM((chunk, chunk), jnp.float32),
            ],
        ),
        compiler_params=pltpu.CompilerParams(vmem_limit_bytes=VMEM),
        cost_estimate=pl.CostEstimate(
            flops=2 * tokens * width * chunk, bytes_accessed=10 * 2**20, transcendentals=tokens
        ),
    )(place, hidden, ids, gain, behind)


def numer_kernel(place_ref, *refs):
    out_ref = refs[4]
    rows = out_ref.shape[1]
    for q_slot in range(4):
        value = refs[q_slot][...].astype(jnp.float32)
        for at, y_slot in enumerate(SLOTS):
            out_ref[place_ref[1] ^ (y_slot * 4 + q_slot)] = value[at * rows : (at + 1) * rows]


def place_numer(place, pieces):
    rows, columns = pieces[0].shape
    rows = rows // 4
    return pl.pallas_call(
        numer_kernel,
        out_shape=jax.ShapeDtypeStruct((16, rows, columns), jnp.float32),
        in_specs=[pl.BlockSpec(memory_space=pltpu.SMEM)]
        + [pl.BlockSpec(memory_space=pltpu.VMEM)] * 4,
        out_specs=pl.BlockSpec(memory_space=pltpu.VMEM),
        compiler_params=pltpu.CompilerParams(vmem_limit_bytes=VMEM),
    )(place, *pieces)


def sums_kernel(place_ref, *refs):
    out_ref = refs[8]
    for gram in range(2):
        for slot in range(4):
            value = refs[gram * 4 + slot][...].astype(jnp.float32)
            rows = value.shape[0] // 4
            row = jnp.concatenate(
                [value[at * rows : (at + 1) * rows] for at in range(4)], axis=1
            )
            chunk = row.shape[1]
            start = pl.multiple_of((place_ref[2] ^ slot) * chunk, 128)
            out_ref[gram, :, pl.ds(start, chunk)] = row


def place_sums(place, pieces):
    rows, share = pieces[0].shape
    return pl.pallas_call(
        sums_kernel,
        out_shape=jax.ShapeDtypeStruct((2, rows // 4, 16 * share), jnp.float32),
        in_specs=[pl.BlockSpec(memory_space=pltpu.SMEM)]
        + [pl.BlockSpec(memory_space=pltpu.VMEM)] * 8,
        out_specs=pl.BlockSpec(memory_space=pltpu.VMEM),
        compiler_params=pltpu.CompilerParams(vmem_limit_bytes=VMEM),
    )(place, *pieces)


def solution(mesh):
    placed = (
        P("mp", "tok"),
        P("mp", "tok", None),
        P("mp", "tok", None),
        P("mp", None, None),
        P("mp", "col", "tok"),
        P("mp", "col", "tok"),
    )
    return jax.shard_map(
        body,
        mesh=mesh,
        in_specs=placed,
        out_specs=(
            P(None, "mp", "tok", "col", None, None),
            P("mp", None, "col", None, "tok"),
            P("mp", None, "col", None, "tok"),
        ),
        check_vma=False,
    )
```
